256 devices in a mesh: ctx: 32 (over z, x), head: 8 (over y, core).
Axes of the slice: x: 4, y: 4, z: 8, core: 2. Of those that a mesh axis runs over, the one named last changes fastest.
Arguments:
- query_states: bfloat16 [16384, 4096], P('ctx', 'head'), may hold values from -12 to 12
- key_states: bfloat16 [16384, 4096], P('ctx', 'head'), may hold values from -12 to 12
- value_states: bfloat16 [16384, 4096], P('ctx', 'head'), may hold values from -6 to 6
- out_weight: bfloat16 [4096, 4096], P('head'), may hold values from -0.5 to 0.5
- doc_reset: int32 [128], P('ctx'), may hold values from 0 to 255
- rand_group: int32 [128, 3], P('ctx'), may hold values from 0 to 31, all different within a row; in each aligned block of 4 rows (0 to 3, 4 to 7, ...) at most 2 rows name the same one
- rand_slot: int32 [128, 3], P('ctx'), may hold values from 0 to 3
- global_blocks: int32 [2], replicated, may hold values from 0 to 127, as said below
Outputs:
- layer_out: bfloat16 [16384, 4096], P(('ctx', 'head'))
The draws below stay inside these ranges and needn't reach their ends.
Inputs may be any that keep to these rules, and one draw needn't show every extreme that they name: `doc_reset`: A value of 128 or more means that no document starts in the block. `rand_group`: the 3 groups of one row differ. In the rows of one device's 4 query blocks no group is named more than 2 times, and in some device's rows some group is named exactly 2 times. `global_blocks`: the 2 global blocks differ, and one of them is the sequence's last block.
All inputs are finite; a program needn't handle non-finite values.
Results may differ from the reference program's by a relative error of at most 0.019.
The reference program's roundings to bfloat16 on the way count: a program that leaves them out, or rounds other values in their place, can miss the bound.
Values may be sent and summed in bfloat16 or wider, within the bound.
A program may use at most 128 MiB of HBM per device.

```python
import math
import jax
import jax.numpy as jnp
import numpy as np
from jax import lax

D = 4096
HEADS = 32
HD = 128
BLK = 128
RAND = 3
GLOB = 2
BLK_DEV = 4
NB = 128
TOKENS = 16384
GROUPS = 32
HEAD_GROUPS = 8
CAP = 2


def paired_states(key):
    base_key = jax.random.fold_in(key, 31)
    subkeys = jax.random.split(base_key, 2)
    array_shape = (TOKENS, HEADS * HD)
    noise_q = jax.random.normal(subkeys[0], array_shape, jnp.float32)
    noise_k = jax.random.normal(subkeys[1], array_shape, jnp.float32)
    query_draw = 1.3 * noise_q
    key_draw = 1.3 * noise_k
    return (jnp.clip(query_draw, -12.0, 12.0), jnp.clip(key_draw, -12.0, 12.0))


def draw_query_states(key, part):
    return paired_states(key)[0].astype(jnp.bfloat16)


def draw_key_states(key, part):
    return paired_states(key)[1].astype(jnp.bfloat16)


def draw_global_blocks(key, part):
    key = jax.random.fold_in(key, 57)
    first_key, second_key = jax.random.split(key)
    other_block = jax.random.randint(first_key, (), 0, NB - 1, dtype=jnp.int32)
    last_block = jnp.int32(NB - 1)
    flipped = jax.random.randint(second_key, (), 0, 2, dtype=jnp.int32)
    pair = jnp.where(flipped == 1, jnp.stack([last_block, other_block]), jnp.stack([other_block, last_block]))
    return pair.astype(jnp.int32)


def place_ends(entries, stream_key, low, high):
    spot = [jax.random.randint(jax.random.fold_in(stream_key, axis), (), 0, length) for axis, length in enumerate(entries.shape)]
    main_axis = entries.shape.index(max(entries.shape))
    beside = spot[:main_axis] + [(spot[main_axis] + 1) % entries.shape[main_axis]] + spot[main_axis + 1:]
    return entries.at[tuple(spot)].set(low).at[tuple(beside)].set(high)


def block_levels(rng, dims, pieces, low, largest):
    def one(dim, parts):
        steps = jax.random.uniform(jax.random.fold_in(jax.random.fold_in(rng, 6), dim), (parts,), jnp.float32, low / len(pieces), largest / len(pieces))
        return jnp.repeat(jnp.exp(steps), dims[dim] // parts).reshape((-1,) + (1,) * (len(dims) - dim - 1))

    factor_of = one(*pieces[0])
    for cut in pieces[1:]:
        factor_of = factor_of * one(*cut)
    return factor_of


def routed_block(stream_key, own, number, rows, count, top, bound, skew):
    order = jax.random.permutation(stream_key, count)
    heavy_load, ordinary = portions_of(count, rows * top, bound, skew, True), portions_of(count, rows * top, bound, skew, False)
    places = jnp.arange(count)

    def named(lengths, turn):
        used = int((lengths > 0).sum())
        fixed = max(1, used // 4)
        moved = fixed + (places - fixed + turn * (used - fixed)) % max(1, count - fixed)
        return jnp.zeros((count,), jnp.int32).at[order[jnp.where(places < fixed, places, moved)]].set(jnp.asarray(lengths, jnp.int32))

    lengths = jnp.where(number % 4 == 0, named(heavy_load, number // 4), named(ordinary, number - number // 4 - 1))
    mixed = jax.random.permutation(jax.random.fold_in(own, 3), count)
    donor, taker = mixed[0:count // 2 * 2:2], mixed[1:count // 2 * 2:2]
    room = jnp.minimum(lengths[donor] - 1, bound - lengths[taker]) // 2
    room = jnp.where((donor == order[0]) | (taker == order[0]) | (lengths[taker] == 0), 0, jnp.maximum(room, 0))
    moved = jax.random.randint(jax.random.fold_in(own, 4), (count // 2,), 0, 1 << 20) % (room + 1)
    lengths = lengths.at[donor].add(-moved).at[taker].add(moved)
    labels = jnp.searchsorted(jnp.cumsum(lengths), jnp.arange(rows * top), side="right").astype(jnp.int32)
    table = labels.reshape(top, rows).T
    table = table[jax.random.permutation(jax.random.fold_in(own, 1), rows)]
    turn = jax.random.randint(jax.random.fold_in(own, 2), (rows, 1), 0, top)
    return jnp.take_along_axis(table, (jnp.arange(top)[None, :] + turn) % top, axis=1)


def portions_of(count, total, most, lean, full):
    loads = [(1 << 20) // math.isqrt(standing ** lean) + 1 for standing in range(1, count + 1)]
    largest = most if full else min(most, max(-(-total // count), total * loads[0] // sum(loads)))
    least = 1 if total - largest >= count - 1 else 0
    given, spare = [largest] + [least] * (count - 1), total - largest - least * (count - 1)
    while spare > 0:
        free = [i for i in range(1, count) if given[i] < largest] or [i for i in range(1, count) if given[i] < most]
        pool, left = sum([loads[i] for i in free]), spare
        for i in free:
            addition = min(most - given[i], max(1, left * loads[i] // pool), spare)
            given[i] = given[i] + addition
            spare = spare - addition
    return np.array(given)


def noise(key, shape, scale, reach, cuts=(), kind=jnp.bfloat16):
    entries = jax.random.normal(key, shape, jnp.float32) * scale
    if len(cuts) > 0:
        entries = block_levels(key, shape, cuts, -0.22, 0.18) * entries
    return jnp.clip(entries, min=-reach, max=reach).astype(kind)


def setup_inputs(seed: int = 0) -> dict:
    key_list = jax.random.split(jax.random.key(seed), 9)
    query_states = draw_query_states(jax.random.fold_in(key_list[8], 71), 0)
    key_states = draw_key_states(jax.random.fold_in(key_list[8], 71), 0)
    value_states = noise(key_list[2], (TOKENS, HEADS * HD), 1.0, 6.0, ((0, 32), (1, 8)))
    out_weight = noise(key_list[3], (HEADS * HD, D), HD ** -0.5, 0.5, ((0, 8),))
    doc_reset = place_ends(jax.random.randint(key_list[4], (NB,), 0, 2 * BLK), jax.random.fold_in(key_list[4], 1), 0, (2 * BLK) - 1).astype(jnp.int32)
    rand_group_keys = jax.random.split(jax.random.fold_in(key_list[5], 1), NB // BLK_DEV)
    rand_group_turns = jax.random.permutation(jax.random.fold_in(key_list[5], 3), NB // BLK_DEV)
    rand_group = jax.vmap(lambda own, number: routed_block(jax.random.fold_in(key_list[5], 2), own, number, BLK_DEV, GROUPS, RAND, CAP, 2))(rand_group_keys, rand_group_turns).reshape((NB, RAND))
    rand_slot = place_ends(jax.random.randint(key_list[6], (NB, RAND), 0, BLK_DEV), jax.random.fold_in(key_list[6], 1), 0, BLK_DEV - 1).astype(jnp.int32)
    global_blocks = draw_global_blocks(jax.random.fold_in(key_list[8], 71), 0)
    return dict(query_states=query_states, key_states=key_states, value_states=value_states, out_weight=out_weight, doc_reset=doc_reset, rand_group=rand_group, rand_slot=rand_slot, global_blocks=global_blocks)


ROPE_BASE = 500000.0


def rope_tables(position, head_dim):
    half_dim = head_dim // 2
    exponent = jnp.arange(half_dim, dtype=jnp.float32) * (2.0 / head_dim)
    inv_freq = jnp.exp(-exponent * math.log(ROPE_BASE))
    angles = position.astype(jnp.float32)[:, None] * inv_freq[None, :]
    return jnp.cos(angles), jnp.sin(angles)


def rotate(states, position, head_dim):
    row_total = states.shape[0]
    half_dim = head_dim // 2
    shaped = states.astype(jnp.float32).reshape(row_total, -1, head_dim)
    cosine, sine_table = rope_tables(position, head_dim)
    cosine = cosine[:, None, :]
    sine_table = sine_table[:, None, :]
    first_half = shaped[..., :half_dim]
    second_half = shaped[..., half_dim:]
    turned = jnp.concatenate([first_half * cosine - second_half * sine_table, second_half * cosine + first_half * sine_table], axis=-1)
    return turned.reshape(row_total, -1).astype(jnp.bfloat16)


def token_positions(doc_reset, block_len):
    block_total = doc_reset.shape[0]
    block_ids = jnp.arange(block_total, dtype=jnp.int32)
    reset_pos = jnp.where(doc_reset < block_len, block_ids * block_len + doc_reset, 0).astype(jnp.int32)
    running = lax.cummax(reset_pos)
    previous = jnp.concatenate([jnp.zeros((1,), jnp.int32), running[:-1]])
    offsets = jnp.arange(block_len, dtype=jnp.int32)
    token_start = jnp.where(offsets[None, :] >= doc_reset[:, None], reset_pos[:, None], previous[:, None])
    tokens = block_ids[:, None] * block_len + offsets[None, :]
    return (tokens - token_start).reshape(-1).astype(jnp.int32)


def part_attention(query_part, key_part, value_part, key_valid, head_dim):
    scores = jnp.einsum("...qhd,...khd->...hqk", query_part.astype(jnp.float32), key_part.astype(jnp.float32)) * (head_dim ** -0.5)
    if key_valid is not None:
        scores = jnp.where(key_valid, scores, -jnp.inf)
    row_max = jnp.max(scores, axis=-1)
    weights = jnp.exp(scores - row_max[..., None]).astype(jnp.bfloat16)
    row_total = jnp.sum(weights.astype(jnp.float32), axis=-1)
    partial_value = jnp.einsum("...hqk,...khd->...qhd", weights.astype(jnp.float32), value_part.astype(jnp.float32)).astype(jnp.bfloat16)
    return row_max, row_total, partial_value


def merge_parts(tops, totals, partials):
    highest = jnp.max(tops, axis=-3, keepdims=True)
    factor = jnp.exp(tops - highest)
    denominator = jnp.sum(factor * totals, axis=-3)
    factor_rows = jnp.swapaxes(factor, -1, -2)[..., None]
    numerator = jnp.sum(factor_rows * partials.astype(jnp.float32), axis=-4)
    merged = numerator / jnp.swapaxes(denominator, -1, -2)[..., None]
    return merged.astype(jnp.bfloat16)


def reference(query_states, key_states, value_states, out_weight, doc_reset, rand_group, rand_slot, global_blocks):
    position = token_positions(doc_reset, BLK)
    rot_q = rotate(query_states, position, HD)
    rot_k = rotate(key_states, position, HD)
    query_tiles = rot_q.reshape(NB, BLK, HEADS, HD)
    key_tiles = rot_k.reshape(NB, BLK, HEADS, HD)
    value_tiles = value_states.reshape(NB, BLK, HEADS, HD)
    global_keys = key_tiles[global_blocks].reshape(GLOB * BLK, HEADS, HD)
    global_values = value_tiles[global_blocks].reshape(GLOB * BLK, HEADS, HD)
    random_ids = (rand_group * BLK_DEV + rand_slot).astype(jnp.int32)

    def one_block(block_num):
        near_ids = jnp.clip(block_num + jnp.arange(-1, 2, dtype=jnp.int32), 0, NB - 1)
        window_keys = key_tiles[near_ids].reshape(3 * BLK, HEADS, HD)
        window_values = value_tiles[near_ids].reshape(3 * BLK, HEADS, HD)
        block_flags = jnp.concatenate([jnp.stack([block_num > 0, block_num >= 0, block_num < NB - 1]), jnp.ones((GLOB,), bool)])
        key_valid = jnp.repeat(block_flags, BLK)[None, None, :]
        query_now = query_tiles[block_num]
        local_part = part_attention(query_now, jnp.concatenate([window_keys, global_keys], 0), jnp.concatenate([window_values, global_values], 0), key_valid, HD)
        chosen = random_ids[block_num]
        query_many = jnp.broadcast_to(query_now[None], (RAND, BLK, HEADS, HD))
        random_part = part_attention(query_many, key_tiles[chosen], value_tiles[chosen], None, HD)
        tops = jnp.concatenate([local_part[0][None], random_part[0]], 0)
        totals = jnp.concatenate([local_part[1][None], random_part[1]], 0)
        partials = jnp.concatenate([local_part[2][None], random_part[2]], 0)
        return merge_parts(tops, totals, partials).reshape(BLK, HEADS * HD)

    attention = lax.map(one_block, jnp.arange(NB, dtype=jnp.int32)).reshape(TOKENS, HEADS * HD)
    group_width = (HEADS // HEAD_GROUPS) * HD
    summed = jnp.zeros((TOKENS, D), jnp.float32)
    for group_num in range(HEAD_GROUPS):
        term = jnp.dot(attention[:, group_num * group_width:(group_num + 1) * group_width], out_weight[group_num * group_width:(group_num + 1) * group_width], preferred_element_type=jnp.float32)
        rounded = lax.optimization_barrier(term.astype(jnp.bfloat16))
        summed = summed + rounded.astype(jnp.float32)
    return summed.astype(jnp.bfloat16)
```

```python
import math

import jax
import jax.numpy as jnp
import numpy as np
from jax import lax
from jax.experimental import pallas as pl
from jax.experimental.pallas import tpu as pltpu
from jax.sharding import PartitionSpec as P

HD = 128
BLK = 128
NZ, NX, NY = 8, 4, 4
GT = 512
WIDTH = 4096
TILE = 512
ROPE_BASE = 500000.0
MESH = pl.DeviceIdType.MESH
F32 = jnp.float32
BF16 = jnp.bfloat16
SCORE_SCALE = HD ** (-0.5) * math.log2(math.e)


def sin_cos(angle):
    turns = jnp.floor(angle * (2.0 / math.pi) + 0.5)
    r = angle - turns * 1.5703125
    r = r - turns * 4.837512969970703125e-4
    r = r - turns * 7.54978995489188216e-8
    quarter = turns - 4.0 * jnp.floor(turns * 0.25)
    z = r * r
    s = r + r * z * (-1.6666654611e-1 + z * (8.3321608736e-3 + z * -1.9515295891e-4))
    c = 1.0 - 0.5 * z + z * z * (
        4.166664568298827e-2 + z * (-1.388731625493765e-3 + z * 2.443315711809948e-5)
    )
    odd = (quarter == 1.0) | (quarter == 3.0)
    sine = jnp.where(odd, c, s)
    cosine = jnp.where(odd, s, c)
    sine = jnp.where(quarter >= 2.0, -sine, sine)
    cosine = jnp.where((quarter == 1.0) | (quarter == 2.0), -cosine, cosine)
    return sine, cosine


def kernel(
    q_hbm, k_hbm, v_hbm, w_hbm, meta_ref, freq_ref, glob_ref, out_ref,
    qin, kin, qrot, krot, qbuf, kbuf, vbuf, wbuf, mall, meta_s, cos_t, sin_t,
    osend, obuf, st1, st2, st3, sa, sb, ra, rb, total,
    in_sem, w_sem, w_send, w_recv,
    mz_send, mz_recv, mx_send, mx_recv, ms_sem,
    z_send, z_recv, x_send, f_send, l_recv, r_recv, f_recv, s_send, s_recv,
    o_send, o_recv, y_send, y_recv,
):
    ctx = lax.axis_index("ctx")
    head = lax.axis_index("head")
    z, x = ctx // NX, ctx % NX
    y, c = head // 2, head % 2
    xr, xl = (x + 1) % NX, (x + NX - 1) % NX
    yr, yl = (y + 1) % NY, (y + NY - 1) % NY
    yo = (y + 2) % NY
    xo = (x + 2) % NX

    def dev(zz, xx, yy, cc):
        return (zz * NX + xx, yy * 2 + cc)

    sib = dev(z, x, y, 1 - c)

    def local(src, dst, sem):
        return pltpu.make_async_copy(src, dst, sem)

    def remote(src, dst, ssem, rsem, to):
        return pltpu.make_async_remote_copy(
            src_ref=src, dst_ref=dst, send_sem=ssem, recv_sem=rsem, device_id=to, device_id_type=MESH
        )

    def arrived(dst, sem):
        pltpu.make_async_copy(dst, dst, sem).wait()

    copy_k = local(k_hbm, kin, in_sem.at[0])
    copy_q = local(q_hbm, qin, in_sem.at[1])
    copy_k.start()
    copy_q.start()

    barrier = pltpu.get_barrier_semaphore()
    for d in range(NZ):
        for e in range(2):
            if d or e:
                pl.semaphore_signal(
                    barrier, inc=1, device_id=dev((z + d) % NZ, x, y, (c + e) % 2), device_id_type=MESH
                )
    for xx in (xr, xl, xo):
        pl.semaphore_signal(barrier, inc=1, device_id=dev(z, xx, y, c), device_id_type=MESH)
    for yy in (yr, yl):
        pl.semaphore_signal(barrier, inc=1, device_id=dev(z, x, yy, c), device_id_type=MESH)
    pl.semaphore_wait(barrier, 2 * NZ - 1 + 3 + 2)

    meta_z = []
    for d in range(1, NZ):
        cp = remote(meta_ref, mall.at[x, z], mz_send.at[d - 1], mz_recv.at[d - 1], dev((z + d) % NZ, x, y, c))
        cp.start()
        meta_z.append(cp)
    mall[x, z] = meta_ref[...]

    def rows_of(group):
        return pl.ds(group * 4, 4)

    own_rows = rows_of(ctx)
    target_core = z % 2

    def z_start(t, j, src, dst):
        row = 4 * c + j
        same = (row == z) & (target_core == c)
        send, recv = z_send.at[t, j], z_recv.at[t, z // 2]

        @pl.when(same)
        def _():
            local(src, dst, recv).start()

        @pl.when(jnp.logical_not(same))
        def _():
            remote(src, dst, send, recv, dev(row, x, y, target_core)).start()

    def z_done(t, j, src, dst):
        row = 4 * c + j
        same = (row == z) & (target_core == c)

        @pl.when(jnp.logical_not(same))
        def _():
            remote(src, dst, z_send.at[t, j], z_recv.at[t, z // 2], dev(row, x, y, target_core)).wait_send()

    q_rows = pl.ds((z // 2) * 4, 4)

    def v_src(j):
        return v_hbm.at[:, :, j * HD : (j + 1) * HD]

    for j in range(4):
        z_start(0, j, v_src(j), vbuf.at[own_rows])

    w_rows = pl.ds(pl.multiple_of(c * GT, GT), GT)
    w_other = pl.ds(pl.multiple_of((1 - c) * GT, GT), GT)
    copy_w = remote(w_hbm, wbuf.at[w_rows], w_send, w_recv, sib)
    copy_w.start()
    keep_w = local(w_hbm, wbuf.at[w_rows], w_sem)
    keep_w.start()

    for cp in meta_z:
        cp.wait_recv()
    meta_x = []
    for d in range(1, NX):
        cp = remote(mall.at[x], mall.at[x], mx_send.at[d - 1], mx_recv.at[d - 1], dev(z, (x + d) % NX, y, c))
        cp.start()
        meta_x.append(cp)
    copy_s = local(mall.at[x], meta_s, ms_sem)
    copy_s.start()
    for cp in meta_x:
        cp.wait_recv()

    doc = mall[:, :, 0, :].astype(F32)
    group_ids = lax.broadcasted_iota(jnp.int32, (NX, NZ, HD), 1) * NX + lax.broadcasted_iota(
        jnp.int32, (NX, NZ, HD), 0
    )
    lane = lax.broadcasted_iota(jnp.int32, (NX, NZ, HD), 2)
    block_ids = group_ids * 4 + lane
    starts = jnp.where((lane < 4) & (doc < float(BLK)), block_ids.astype(F32) * float(BLK) + doc, 0.0)
    own_doc = meta_ref[0:1, :].astype(F32)
    offset = lax.broadcasted_iota(jnp.int32, (BLK, HD), 0).astype(F32)
    half_sign = jnp.where(lax.broadcasted_iota(jnp.int32, (BLK, HD), 1) < HD // 2, -1.0, 1.0)
    for b in range(4):
        block = ctx * 4 + b
        before = jnp.where(block_ids < block, starts, 0.0)
        before = jnp.max(jnp.max(before, axis=0), axis=0, keepdims=True)
        before = jnp.max(before, axis=1, keepdims=True)
        reset = own_doc[0:1, b : b + 1]
        first = (block * BLK).astype(F32)
        begin = jnp.where(offset >= reset, first + reset, before)
        angle = (first + offset - begin) * freq_ref[0:1, :]
        sine, cosine = sin_cos(angle)
        cos_t[b * BLK : (b + 1) * BLK, :] = cosine
        sin_t[b * BLK : (b + 1) * BLK, :] = sine * half_sign

    def rotate(src, dst, j):
        @pl.loop(0, 4)
        def _(b):
            rows = pl.ds(pl.multiple_of(b * BLK, BLK), BLK)
            value = src[rows, j * HD : (j + 1) * HD].astype(F32)
            turned = value * cos_t[rows, :] + pltpu.roll(value, HD // 2, 1) * sin_t[rows, :]
            dst[j, b] = turned.astype(BF16)

    copy_k.wait()
    for j in range(4):
        rotate(kin, krot, j)
        z_start(1, j, krot.at[j], kbuf.at[own_rows])

    bufs = (vbuf, kbuf)

    def group_from(i, xx):
        return (2 * i + c) * NX + xx

    def x_out(t, i, k, to_x, recv):
        piece = bufs[t].at[rows_of(group_from(i, x))]
        return remote(piece, piece, x_send.at[t, i, k], recv.at[t, i], dev(z, to_x, y, c))

    def share(t, k, i, xx):
        piece = bufs[t].at[rows_of(group_from(i, xx))]
        return remote(piece, piece, s_send.at[t, k, i], s_recv.at[t, k, i], sib)

    def forward(t, i):
        from_x = jnp.where(c == 0, xl, xr)
        to_x = jnp.where(c == 0, xr, xl)
        piece = bufs[t].at[rows_of(group_from(i, from_x))]
        return remote(piece, piece, f_send.at[t, i], f_recv.at[t, i], dev(z, to_x, y, c))

    def own_step(t):
        @pl.loop(0, 4)
        def _(i):
            arrived(bufs[t].at[rows_of(group_from(i, x))], z_recv.at[t, i])
            x_out(t, i, 0, xr, l_recv).start()
            x_out(t, i, 1, xl, r_recv).start()
            share(t, 0, i, x).start()

    def side_step(t):
        @pl.loop(0, 4)
        def _(i):
            arrived(bufs[t].at[rows_of(group_from(i, xl))], l_recv.at[t, i])

            @pl.when(c == 0)
            def _():
                forward(t, i).start()

            share(t, 1, i, xl).start()
            arrived(bufs[t].at[rows_of(group_from(i, xr))], r_recv.at[t, i])

            @pl.when(c == 1)
            def _():
                forward(t, i).start()

            share(t, 2, i, xr).start()

    def far_step(t):
        @pl.loop(0, 4)
        def _(i):
            arrived(bufs[t].at[rows_of(group_from(i, xo))], f_recv.at[t, i])
            share(t, 3, i, xo).start()

    own_step(0)
    copy_q.wait()
    for j in range(4):
        rotate(qin, qrot, j)
        z_start(2, j, qrot.at[j], qbuf.at[q_rows])
    side_step(0)
    own_step(1)
    far_step(0)
    side_step(1)
    far_step(1)

    def from_sibling(t):
        @pl.loop(0, 4)
        def _(i):
            group = (2 * i + 1 - c) * NX
            for k, xx in enumerate((x, xl, xr, xo)):
                arrived(bufs[t].at[rows_of(group + xx)], s_recv.at[t, k, i])

    from_sibling(0)
    from_sibling(1)

    @pl.loop(0, 4)
    def _(i):
        arrived(qbuf.at[pl.ds(i * 4, 4)], z_recv.at[2, i])

    copy_s.wait()

    ones = jnp.ones((8 * BLK, HD), BF16)
    order = (yo, yr, yl, y)

    def o_copies(step, b, i):
        zz = 2 * i + c
        for e in range(2):
            src = osend.at[step, i, pl.ds(e * 64, 64)]
            dst = obuf.at[b * NZ + z]
            yield e, (zz == z) & (c == e), src, dst, dev(zz, x, y, e)

    def attend(step):
        b = order[step]

        @pl.loop(0, 4)
        def _(i):
            zz = 2 * i + c
            block = (zz * NX + x) * 4 + b
            ids = [
                jnp.maximum(block - 1, 0),
                block,
                jnp.minimum(block + 1, 127),
                glob_ref[0],
                glob_ref[1],
                meta_s[zz, 0, 4 + b * 3],
                meta_s[zz, 0, 5 + b * 3],
                meta_s[zz, 0, 6 + b * 3],
            ]
            q = qbuf[i * 4 + b]
            keys = jnp.concatenate([kbuf[n] for n in ids], axis=0)
            scores = lax.dot_general(q, keys, (((1,), (1,)), ((), ())), preferred_element_type=F32)
            low = jnp.where(block > 0, 0.0, -1e30).astype(F32)
            high = jnp.where(block < 127, 0.0, -1e30).astype(F32)
            scores = jnp.concatenate(
                [
                    scores[:, :BLK] + low,
                    scores[:, BLK : 2 * BLK],
                    scores[:, 2 * BLK : 3 * BLK] + high,
                    scores[:, 3 * BLK :],
                ],
                axis=1,
            ) * SCORE_SCALE
            top = jnp.max(scores, axis=1, keepdims=True)
            weights = jnp.exp2(scores - top).astype(BF16)
            values = jnp.concatenate([vbuf[n] for n in ids], axis=0)
            both = jnp.dot(weights, jnp.concatenate([values, ones], axis=1), preferred_element_type=F32)
            osend[step, i] = (both[:, :HD] / both[:, HD:]).astype(BF16)
            for e, same, src, dst, to in o_copies(step, b, i):

                @pl.when(same)
                def _():
                    local(src, dst, o_recv.at[step]).start()

                @pl.when(jnp.logical_not(same))
                def _():
                    remote(src, dst, o_send.at[step, i, e], o_recv.at[step], to).start()

    def outputs_of(step):
        b = order[step]
        arrived(obuf.at[pl.ds(b * NZ, NZ)], o_recv.at[step])
        return b

    def project(b, first, last, finish):
        @pl.loop(first, last)
        def _(n):
            cols = pl.ds(pl.multiple_of(n * TILE, TILE), TILE)
            rows = jnp.concatenate([obuf[b * NZ + m] for m in range(NZ)], axis=1)
            finish(cols, jnp.dot(rows, wbuf[:, cols], preferred_element_type=F32))

    half = WIDTH // 2
    tiles = WIDTH // TILE
    left, right = pl.ds(0, half), pl.ds(half, half)

    def y_copy(k, src, dst, yy):
        return remote(src, dst, y_send.at[k], y_recv.at[k], dev(z, x, yy, c))

    y_copies = [
        y_copy(0, st1.at[:, left], sa, yr),
        y_copy(1, st1.at[:, right], sb, yl),
        y_copy(2, st2.at[:, right], ra.at[:, right], yr),
        y_copy(3, st2.at[:, left], ra.at[:, left], yr),
        y_copy(4, st3.at[:, left], rb.at[:, left], yl),
        y_copy(5, st3.at[:, right], rb.at[:, right], yl),
    ]

    def put(ref):
        def finish(cols, tile):
            ref[:, cols] = tile.astype(ref.dtype)

        return finish

    def project_0():
        b = outputs_of(0)
        project(b, 0, tiles // 2, put(st1))
        y_copies[0].start()
        project(b, tiles // 2, tiles, put(st1))
        y_copies[1].start()

    def project_1():
        b = outputs_of(1)
        project(b, tiles // 2, tiles, put(st2))
        y_copies[2].start()
        y_copies[0].wait_recv()

        def finish(cols, tile):
            st2[:, cols] = (tile + sa[:, cols].astype(F32)).astype(BF16)

        project(b, 0, tiles // 2, finish)
        y_copies[3].start()

    def project_2():
        b = outputs_of(2)
        project(b, 0, tiles // 2, put(st3))
        y_copies[4].start()
        y_copies[1].wait_recv()

        @pl.loop(tiles // 2, tiles)
        def _(n):
            cols = pl.ds(pl.multiple_of(n * TILE, TILE), TILE)
            near = pl.ds(pl.multiple_of(n * TILE - half, TILE), TILE)
            rows = jnp.concatenate([obuf[b * NZ + m] for m in range(NZ)], axis=1)
            tile = jnp.dot(rows, wbuf[:, cols], preferred_element_type=F32)
            st3[:, cols] = (tile + sb[:, near].astype(F32)).astype(BF16)

        y_copies[5].start()

    def project_3():
        b = outputs_of(3)
        project(b, 0, tiles, put(total))

    attend(0)
    attend(1)
    keep_w.wait()
    copy_w.wait_send()
    arrived(wbuf.at[w_other], w_recv)
    project_0()
    attend(2)
    project_1()
    attend(3)
    project_2()
    project_3()
    for k in (2, 3, 4, 5):
        y_copies[k].wait_recv()

    @pl.loop(0, tiles)
    def _(n):
        cols = pl.ds(pl.multiple_of(n * TILE, TILE), TILE)
        out_ref[:, cols] = (total[:, cols] + ra[:, cols].astype(F32) + rb[:, cols].astype(F32)).astype(BF16)

    for cp in meta_z:
        cp.wait_send()
    for cp in meta_x:
        cp.wait_send()
    for j in range(4):
        z_done(0, j, v_src(j), vbuf.at[own_rows])
        z_done(1, j, krot.at[j], kbuf.at[own_rows])
        z_done(2, j, qrot.at[j], qbuf.at[q_rows])
    for t in range(2):

        @pl.loop(0, 4)
        def _(i):
            x_out(t, i, 0, xr, l_recv).wait_send()
            x_out(t, i, 1, xl, r_recv).wait_send()
            forward(t, i).wait_send()
            for k, xx in enumerate((x, xl, xr, xo)):
                share(t, k, i, xx).wait_send()

    for step in range(4):

        @pl.loop(0, 4)
        def _(i):
            for e, same, src, dst, to in o_copies(step, order[step], i):

                @pl.when(jnp.logical_not(same))
                def _():
                    remote(src, dst, o_send.at[step, i, e], o_recv.at[step], to).wait_send()

    for cp in y_copies:
        cp.wait_send()


def on_device(q, k, v, w, doc_reset, rand_group, rand_slot, global_blocks):
    numbers = jnp.concatenate([doc_reset, (rand_group * 4 + rand_slot).reshape(-1)])
    meta = jnp.broadcast_to(jnp.pad(numbers, (0, HD - numbers.shape[0]))[None], (8, HD))
    pair = np.arange(HD // 2, dtype=np.float64) * (2.0 / HD)
    freq = np.exp(-pair * math.log(ROPE_BASE)).astype(np.float32)
    freq = jnp.asarray(np.broadcast_to(np.concatenate([freq, freq])[None], (8, HD)).copy())
    vmem = pltpu.VMEM
    dma = pltpu.SemaphoreType.DMA
    any_spec = pl.BlockSpec(memory_space=pl.ANY)
    vmem_spec = pl.BlockSpec(memory_space=pltpu.VMEM)
    return pl.pallas_call(
        kernel,
        out_shape=jax.ShapeDtypeStruct((64, WIDTH), BF16),
        in_specs=[any_spec] * 4 + [vmem_spec] * 2 + [pl.BlockSpec(memory_space=pltpu.SMEM)],
        out_specs=vmem_spec,
        scratch_shapes=[
            vmem((GT, GT), BF16),
            vmem((GT, GT), BF16),
            vmem((4, 4, BLK, HD), BF16),
            vmem((4, 4, BLK, HD), BF16),
            vmem((16, BLK, HD), BF16),
            vmem((128, BLK, HD), BF16),
            vmem((128, BLK, HD), BF16),
            vmem((2 * GT, WIDTH), BF16),
            vmem((NX, NZ, 8, HD), jnp.int32),
            pltpu.SMEM((NZ, 8, HD), jnp.int32),
            vmem((GT, HD), F32),
            vmem((GT, HD), F32),
            vmem((4, 4, BLK, HD), BF16),
            vmem((4 * NZ, 64, HD), BF16),
            vmem((64, WIDTH), BF16),
            vmem((64, WIDTH), BF16),
            vmem((64, WIDTH), BF16),
            vmem((64, WIDTH // 2), BF16),
            vmem((64, WIDTH // 2), BF16),
            vmem((64, WIDTH), BF16),
            vmem((64, WIDTH), BF16),
            vmem((64, WIDTH), F32),
            dma((2,)), dma, dma, dma,
            dma((NZ - 1,)), dma((NZ - 1,)), dma((NX - 1,)), dma((NX - 1,)), dma,
            dma((3, 4)), dma((3, 4)), dma((2, 4, 2)), dma((2, 4)),
            dma((2, 4)), dma((2, 4)), dma((2, 4)), dma((2, 4, 4)), dma((2, 4, 4)),
            dma((4, 4, 2)), dma((4,)), dma((6,)), dma((6,)),
        ],
        compiler_params=pltpu.CompilerParams(
            collective_id=0, has_side_effects=True, vmem_limit_bytes=48 << 20
        ),
        cost_estimate=pl.CostEstimate(flops=3_300_000_000, bytes_accessed=8 << 20, transcendentals=2_200_000),
    )(q, k, v.reshape(4, BLK, GT), w, meta, freq, global_blocks)


def solution(mesh):
    placed = (
        P("ctx", "head"),
        P("ctx", "head"),
        P("ctx", "head"),
        P("head", None),
        P("ctx"),
        P("ctx", None),
        P("ctx", None),
        P(),
    )
    return jax.shard_map(
        on_device, mesh=mesh, in_specs=placed, out_specs=P(("ctx", "head"), None), check_vma=False
    )
```

```python
import math

import jax
import jax.numpy as jnp
import numpy as np
from jax import lax
from jax.experimental import pallas as pl
from jax.experimental.pallas import tpu as pltpu
from jax.sharding import PartitionSpec as P

HD = 128
BLK = 128
NZ, NX, NY = 8, 4, 4
GT = 512
WIDTH = 4096
TILE = 512
ROPE_BASE = 500000.0
MESH = pl.DeviceIdType.MESH
F32 = jnp.float32
BF16 = jnp.bfloat16
SCORE_SCALE = HD ** (-0.5) * math.log2(math.e)


def sin_cos(angle):
    turns = jnp.floor(angle * (2.0 / math.pi) + 0.5)
    r = angle - turns * 1.5703125
    r = r - turns * 4.837512969970703125e-4
    r = r - turns * 7.54978995489188216e-8
    quarter = turns - 4.0 * jnp.floor(turns * 0.25)
    z = r * r
    s = r + r * z * (-1.6666654611e-1 + z * (8.3321608736e-3 + z * -1.9515295891e-4))
    c = 1.0 - 0.5 * z + z * z * (
        4.166664568298827e-2 + z * (-1.388731625493765e-3 + z * 2.443315711809948e-5)
    )
    odd = (quarter == 1.0) | (quarter == 3.0)
    sine = jnp.where(odd, c, s)
    cosine = jnp.where(odd, s, c)
    sine = jnp.where(quarter >= 2.0, -sine, sine)
    cosine = jnp.where((quarter == 1.0) | (quarter == 2.0), -cosine, cosine)
    return sine, cosine


def code(*digits):
    return sum(d * 4**k for k, d in enumerate(digits))


def kernel(
    q_hbm, k_hbm, v_hbm, w_hbm, freq_ref, doc_ref, group_ref, slot_ref, glob_ref, out_ref,
    meta_ref, qin, kin, qrot, krot, qbuf, kbuf, vbuf, wbuf, mall, meta_s, cos_t, sin_t,
    osend, obuf, st1, st2, st3, sa, sb, ra, rb, total,
    in_sem, w_sem, w_send, w_recv,
    mz_send, mz_recv, mx_send, mx_recv, ms_sem,
    z_send, z_recv, x_send, f_send, l_recv, r_recv, f_recv, s_send, s_recv,
    o_send, o_recv, y_send, y_recv,
):
    ctx = lax.axis_index("ctx")
    head = lax.axis_index("head")
    z, x = ctx // NX, ctx % NX
    y, c = head // 2, head % 2
    xr, xl = (x + 1) % NX, (x + NX - 1) % NX
    yr, yl = (y + 1) % NY, (y + NY - 1) % NY
    yo = (y + 2) % NY
    xo = (x + 2) % NX

    def dev(zz, xx, yy, cc):
        return (zz * NX + xx, yy * 2 + cc)

    sib = dev(z, x, y, 1 - c)

    def local(src, dst, sem):
        return pltpu.make_async_copy(src, dst, sem)

    def remote(src, dst, ssem, rsem, to):
        return pltpu.make_async_remote_copy(
            src_ref=src, dst_ref=dst, send_sem=ssem, recv_sem=rsem, device_id=to, device_id_type=MESH
        )

    def arrived(dst, sem):
        pltpu.make_async_copy(dst, dst, sem).wait()

    copy_k = local(k_hbm, kin, in_sem.at[0])
    copy_q = local(q_hbm, qin, in_sem.at[1])
    copy_k.start()
    copy_q.start()

    numbers = [doc_ref[b] for b in range(4)]
    numbers += [group_ref[b, n] * 4 + slot_ref[b, n] for b in range(4) for n in range(3)]
    spot = lax.broadcasted_iota(jnp.int32, (8, HD), 1)
    packed = jnp.zeros((8, HD), jnp.int32)
    for n, number in enumerate(numbers):
        packed = jnp.where(spot == n, number, packed)
    meta_ref[...] = packed

    barrier = pltpu.get_barrier_semaphore()
    for d in range(NZ):
        for e in range(2):
            if d or e:
                pl.semaphore_signal(
                    barrier, inc=1, device_id=dev((z + d) % NZ, x, y, (c + e) % 2), device_id_type=MESH
                )
    for xx in (xr, xl, xo):
        pl.semaphore_signal(barrier, inc=1, device_id=dev(z, xx, y, c), device_id_type=MESH)
    for yy in (yr, yl):
        pl.semaphore_signal(barrier, inc=1, device_id=dev(z, x, yy, c), device_id_type=MESH)
    pl.semaphore_wait(barrier, 2 * NZ - 1 + 3 + 2)

    meta_z = []
    for d in range(1, NZ):
        cp = remote(meta_ref, mall.at[x, z], mz_send.at[d - 1], mz_recv.at[d - 1], dev((z + d) % NZ, x, y, c))
        cp.start()
        meta_z.append(cp)
    mall[x, z] = meta_ref[...]

    def rows_of(group):
        return pl.ds(group * 4, 4)

    own_rows = rows_of(ctx)
    target_core = z % 2

    place = z % 4
    near = jnp.where(
        place == 0, code(0, 1, 2, 3),
        jnp.where(place == 1, code(1, 0, 2, 3), jnp.where(place == 2, code(2, 3, 1, 0), code(3, 2, 1, 0))),
    )
    far = jnp.where(
        place == 0, code(3, 2, 1, 0),
        jnp.where(place == 1, code(3, 2, 0, 1), jnp.where(place == 2, code(0, 1, 3, 2), code(0, 1, 2, 3))),
    )
    targets = jnp.where(z // 4 == c, near, far)
    target = [(targets // 4**k) % 4 for k in range(4)]
    nearest = (z - c + 1) // 2 + 4
    sender = [(nearest + d) % 4 for d in (0, 3, 1, 2)]

    def z_start(t, j, src, dst):
        row = 4 * c + j
        same = (row == z) & (target_core == c)
        send, recv = z_send.at[t, j], z_recv.at[t, z // 2]

        @pl.when(same)
        def _():
            local(src, dst, recv).start()

        @pl.when(jnp.logical_not(same))
        def _():
            remote(src, dst, send, recv, dev(row, x, y, target_core)).start()

    def z_done(t, j, src, dst):
        row = 4 * c + j
        same = (row == z) & (target_core == c)

        @pl.when(jnp.logical_not(same))
        def _():
            remote(src, dst, z_send.at[t, j], z_recv.at[t, z // 2], dev(row, x, y, target_core)).wait_send()

    q_rows = pl.ds((z // 2) * 4, 4)

    def v_src(j):
        return v_hbm.at[:, :, pl.ds(pl.multiple_of(j * HD, HD), HD)]

    bufs = (vbuf, kbuf)

    def group_from(i, xx):
        return (2 * i + c) * NX + xx

    def x_out(t, i, k, to_x, recv):
        piece = bufs[t].at[rows_of(group_from(i, x))]
        return remote(piece, piece, x_send.at[t, i, k], recv.at[t, i], dev(z, to_x, y, c))

    def share(t, k, i, xx):
        piece = bufs[t].at[rows_of(group_from(i, xx))]
        return remote(piece, piece, s_send.at[t, k, i], s_recv.at[t, k, i], sib)

    def forward(t, i):
        from_x = jnp.where(c == 0, xl, xr)
        to_x = jnp.where(c == 0, xr, xl)
        piece = bufs[t].at[rows_of(group_from(i, from_x))]
        return remote(piece, piece, f_send.at[t, i], f_recv.at[t, i], dev(z, to_x, y, c))

    def own_step(t, n):
        i = sender[n]
        arrived(bufs[t].at[rows_of(group_from(i, x))], z_recv.at[t, i])
        x_out(t, i, 0, xr, l_recv).start()
        x_out(t, i, 1, xl, r_recv).start()
        share(t, 0, i, x).start()

    def side_step(t, n):
        i = sender[n]
        arrived(bufs[t].at[rows_of(group_from(i, xl))], l_recv.at[t, i])

        @pl.when(c == 0)
        def _():
            forward(t, i).start()

        arrived(bufs[t].at[rows_of(group_from(i, xr))], r_recv.at[t, i])

        @pl.when(c == 1)
        def _():
            forward(t, i).start()

        share(t, 1, i, xl).start()
        share(t, 2, i, xr).start()

    def far_step(t, n):
        i = sender[n]
        arrived(bufs[t].at[rows_of(group_from(i, xo))], f_recv.at[t, i])
        share(t, 3, i, xo).start()

    for j in target:
        z_start(0, j, v_src(j), vbuf.at[own_rows])
    own_step(0, 0)

    for cp in meta_z:
        cp.wait_recv()
    meta_x = []
    for d in range(1, NX):
        cp = remote(mall.at[x], mall.at[x], mx_send.at[d - 1], mx_recv.at[d - 1], dev(z, (x + d) % NX, y, c))
        cp.start()
        meta_x.append(cp)
    copy_s = local(mall.at[x], meta_s, ms_sem)
    copy_s.start()
    own_step(0, 1)
    for cp in meta_x:
        cp.wait_recv()

    doc = mall[:, :, 0, :].astype(F32)
    group_ids = lax.broadcasted_iota(jnp.int32, (NX, NZ, HD), 1) * NX + lax.broadcasted_iota(
        jnp.int32, (NX, NZ, HD), 0
    )
    lane = lax.broadcasted_iota(jnp.int32, (NX, NZ, HD), 2)
    block_ids = group_ids * 4 + lane
    starts = jnp.where((lane < 4) & (doc < float(BLK)), block_ids.astype(F32) * float(BLK) + doc, 0.0)
    own_doc = meta_ref[0:1, :].astype(F32)
    offset = lax.broadcasted_iota(jnp.int32, (BLK, HD), 0).astype(F32)
    half_sign = jnp.where(lax.broadcasted_iota(jnp.int32, (BLK, HD), 1) < HD // 2, -1.0, 1.0)
    for b in range(4):
        block = ctx * 4 + b
        before = jnp.where(block_ids < block, starts, 0.0)
        before = jnp.max(jnp.max(before, axis=0), axis=0, keepdims=True)
        before = jnp.max(before, axis=1, keepdims=True)
        reset = own_doc[0:1, b : b + 1]
        first = (block * BLK).astype(F32)
        begin = jnp.where(offset >= reset, first + reset, before)
        angle = (first + offset - begin) * freq_ref[0:1, :]
        sine, cosine = sin_cos(angle)
        cos_t[b * BLK : (b + 1) * BLK, :] = cosine
        sin_t[b * BLK : (b + 1) * BLK, :] = sine * half_sign

    def rotate(src, dst, j):
        for b in range(4):
            rows = pl.ds(b * BLK, BLK)
            value = src[rows, j * HD : (j + 1) * HD].astype(F32)
            turned = value * cos_t[rows, :] + pltpu.roll(value, HD // 2, 1) * sin_t[rows, :]
            dst[j, b] = turned.astype(BF16)

    copy_k.wait()
    for j in range(4):
        rotate(kin, krot, j)
    for j in target:
        z_start(1, j, krot.at[j], kbuf.at[own_rows])
    own_step(0, 2)
    own_step(0, 3)
    copy_q.wait()
    for j in range(4):
        rotate(qin, qrot, j)

    own_step(1, 0)
    for j in target:
        z_start(2, j, qrot.at[j], qbuf.at[q_rows])
    w_rows = pl.ds(pl.multiple_of(c * GT, GT), GT)
    w_other = pl.ds(pl.multiple_of((1 - c) * GT, GT), GT)
    copy_w = remote(w_hbm, wbuf.at[w_rows], w_send, w_recv, sib)
    copy_w.start()
    keep_w = local(w_hbm, wbuf.at[w_rows], w_sem)
    keep_w.start()

    side_step(0, 0)
    for n in range(1, 4):
        own_step(1, n)
        side_step(0, n)
    for n in range(4):
        side_step(1, n)
        far_step(0, n)
    for n in range(4):
        far_step(1, n)

    def from_sibling(t):
        @pl.loop(0, 4)
        def _(i):
            group = (2 * i + 1 - c) * NX
            for k, xx in enumerate((x, xl, xr, xo)):
                arrived(bufs[t].at[rows_of(group + xx)], s_recv.at[t, k, i])

    from_sibling(0)
    from_sibling(1)

    @pl.loop(0, 4)
    def _(i):
        arrived(qbuf.at[pl.ds(i * 4, 4)], z_recv.at[2, i])

    copy_s.wait()

    ones = jnp.ones((8 * BLK, HD), BF16)
    order = (yo, yr, yl, y)

    def o_copies(step, b, i):
        zz = 2 * i + c
        for e in range(2):
            src = osend.at[step, i, pl.ds(e * 64, 64)]
            dst = obuf.at[b * NZ + z]
            yield e, (zz == z) & (c == e), src, dst, dev(zz, x, y, e)

    def attend(step):
        b = order[step]

        @pl.loop(0, 4, unroll=True)
        def _(i):
            zz = 2 * i + c
            block = (zz * NX + x) * 4 + b
            ids = [
                jnp.maximum(block - 1, 0),
                block,
                jnp.minimum(block + 1, 127),
                glob_ref[0],
                glob_ref[1],
                meta_s[zz, 0, 4 + b * 3],
                meta_s[zz, 0, 5 + b * 3],
                meta_s[zz, 0, 6 + b * 3],
            ]
            q = qbuf[i * 4 + b]
            keys = jnp.concatenate([kbuf[n] for n in ids], axis=0)
            scores = lax.dot_general(q, keys, (((1,), (1,)), ((), ())), preferred_element_type=F32)
            low = jnp.where(block > 0, 0.0, -1e30).astype(F32)
            high = jnp.where(block < 127, 0.0, -1e30).astype(F32)
            scores = jnp.concatenate(
                [
                    scores[:, :BLK] + low,
                    scores[:, BLK : 2 * BLK],
                    scores[:, 2 * BLK : 3 * BLK] + high,
                    scores[:, 3 * BLK :],
                ],
                axis=1,
            ) * SCORE_SCALE
            top = jnp.max(scores, axis=1, keepdims=True)
            weights = jnp.exp2(scores - top).astype(BF16)
            values = jnp.concatenate([vbuf[n] for n in ids], axis=0)
            both = jnp.dot(weights, jnp.concatenate([values, ones], axis=1), preferred_element_type=F32)
            osend[step, i] = (both[:, :HD] / both[:, HD:]).astype(BF16)
            for e, same, src, dst, to in o_copies(step, b, i):

                @pl.when(same)
                def _():
                    local(src, dst, o_recv.at[step]).start()

                @pl.when(jnp.logical_not(same))
                def _():
                    remote(src, dst, o_send.at[step, i, e], o_recv.at[step], to).start()

    def outputs_of(step):
        b = order[step]
        arrived(obuf.at[pl.ds(b * NZ, NZ)], o_recv.at[step])
        return b

    def project(b, first, last, finish):
        @pl.loop(first, last, unroll=True)
        def _(n):
            cols = pl.ds(pl.multiple_of(n * TILE, TILE), TILE)
            rows = jnp.concatenate([obuf[b * NZ + m] for m in range(NZ)], axis=1)
            finish(cols, jnp.dot(rows, wbuf[:, cols], preferred_element_type=F32))

    half = WIDTH // 2
    tiles = WIDTH // TILE
    left, right = pl.ds(0, half), pl.ds(half, half)

    def y_copy(k, src, dst, yy):
        return remote(src, dst, y_send.at[k], y_recv.at[k], dev(z, x, yy, c))

    y_copies = [
        y_copy(0, st1.at[:, left], sa, yr),
        y_copy(1, st1.at[:, right], sb, yl),
        y_copy(2, st2.at[:, right], ra.at[:, right], yr),
        y_copy(3, st2.at[:, left], ra.at[:, left], yr),
        y_copy(4, st3.at[:, left], rb.at[:, left], yl),
        y_copy(5, st3.at[:, right], rb.at[:, right], yl),
    ]

    def put(ref):
        def finish(cols, tile):
            ref[:, cols] = tile.astype(ref.dtype)

        return finish

    def project_0():
        b = outputs_of(0)
        project(b, 0, tiles // 2, put(st1))
        y_copies[0].start()
        project(b, tiles // 2, tiles, put(st1))
        y_copies[1].start()

    def project_1_near():
        b = outputs_of(1)
        project(b, tiles // 2, tiles, put(st2))

    def project_1_far():
        def finish(cols, tile):
            st2[:, cols] = (tile + sa[:, cols].astype(F32)).astype(BF16)

        y_copies[0].wait_recv()
        project(order[1], 0, tiles // 2, finish)
        y_copies[3].start()

    def project_2_near():
        b = outputs_of(2)
        project(b, 0, tiles // 2, put(st3))

    def project_2_far():
        y_copies[1].wait_recv()
        b = order[2]

        @pl.loop(tiles // 2, tiles, unroll=True)
        def _(n):
            cols = pl.ds(pl.multiple_of(n * TILE, TILE), TILE)
            near = pl.ds(pl.multiple_of(n * TILE - half, TILE), TILE)
            rows = jnp.concatenate([obuf[b * NZ + m] for m in range(NZ)], axis=1)
            tile = jnp.dot(rows, wbuf[:, cols], preferred_element_type=F32)
            st3[:, cols] = (tile + sb[:, near].astype(F32)).astype(BF16)

        y_copies[5].start()

    def project_3():
        b = outputs_of(3)
        project(b, 0, tiles, put(total))

    attend(0)
    attend(1)
    keep_w.wait()
    copy_w.wait_send()
    arrived(wbuf.at[w_other], w_recv)
    attend(2)
    project_0()
    project_1_near()
    attend(3)
    y_copies[0].wait_send()
    y_copies[2].start()
    project_2_near()
    y_copies[1].wait_send()
    y_copies[4].start()
    project_1_far()
    project_2_far()
    project_3()
    for k in (2, 3, 4, 5):
        y_copies[k].wait_recv()

    @pl.loop(0, tiles)
    def _(n):
        cols = pl.ds(pl.multiple_of(n * TILE, TILE), TILE)
        out_ref[:, cols] = (total[:, cols] + ra[:, cols].astype(F32) + rb[:, cols].astype(F32)).astype(BF16)

    for cp in meta_z:
        cp.wait_send()
    for cp in meta_x:
        cp.wait_send()
    for j in range(4):
        z_done(0, j, v_src(j), vbuf.at[own_rows])
        z_done(1, j, krot.at[j], kbuf.at[own_rows])
        z_done(2, j, qrot.at[j], qbuf.at[q_rows])
    for t in range(2):

        @pl.loop(0, 4)
        def _(i):
            x_out(t, i, 0, xr, l_recv).wait_send()
            x_out(t, i, 1, xl, r_recv).wait_send()
            forward(t, i).wait_send()
            for k, xx in enumerate((x, xl, xr, xo)):
                share(t, k, i, xx).wait_send()

    for step in range(4):

        @pl.loop(0, 4)
        def _(i):
            for e, same, src, dst, to in o_copies(step, order[step], i):

                @pl.when(jnp.logical_not(same))
                def _():
                    remote(src, dst, o_send.at[step, i, e], o_recv.at[step], to).wait_send()

    for cp in y_copies[2:]:
        cp.wait_send()


def on_device(q, k, v, w, doc_reset, rand_group, rand_slot, global_blocks):
    pair = np.arange(HD // 2, dtype=np.float64) * (2.0 / HD)
    freq = np.exp(-pair * math.log(ROPE_BASE)).astype(np.float32)
    freq = jnp.asarray(np.broadcast_to(np.concatenate([freq, freq])[None], (8, HD)).copy())
    vmem = pltpu.VMEM
    dma = pltpu.SemaphoreType.DMA
    any_spec = pl.BlockSpec(memory_space=pl.ANY)
    vmem_spec = pl.BlockSpec(memory_space=pltpu.VMEM)
    return pl.pallas_call(
        kernel,
        out_shape=jax.ShapeDtypeStruct((64, WIDTH), BF16),
        in_specs=[any_spec] * 4 + [vmem_spec] + [pl.BlockSpec(memory_space=pltpu.SMEM)] * 4,
        out_specs=vmem_spec,
        scratch_shapes=[
            vmem((8, HD), jnp.int32),
            vmem((GT, GT), BF16),
            vmem((GT, GT), BF16),
            vmem((4, 4, BLK, HD), BF16),
            vmem((4, 4, BLK, HD), BF16),
            vmem((16, BLK, HD), BF16),
            vmem((128, BLK, HD), BF16),
            vmem((128, BLK, HD), BF16),
            vmem((2 * GT, WIDTH), BF16),
            vmem((NX, NZ, 8, HD), jnp.int32),
            pltpu.SMEM((NZ, 8, HD), jnp.int32),
            vmem((GT, HD), F32),
            vmem((GT, HD), F32),
            vmem((4, 4, BLK, HD), BF16),
            vmem((4 * NZ, 64, HD), BF16),
            vmem((64, WIDTH), BF16),
            vmem((64, WIDTH), BF16),
            vmem((64, WIDTH), BF16),
            vmem((64, WIDTH // 2), BF16),
            vmem((64, WIDTH // 2), BF16),
            vmem((64, WIDTH), BF16),
            vmem((64, WIDTH), BF16),
            vmem((64, WIDTH), F32),
            dma((2,)), dma, dma, dma,
            dma((NZ - 1,)), dma((NZ - 1,)), dma((NX - 1,)), dma((NX - 1,)), dma,
            dma((3, 4)), dma((3, 4)), dma((2, 4, 2)), dma((2, 4)),
            dma((2, 4)), dma((2, 4)), dma((2, 4)), dma((2, 4, 4)), dma((2, 4, 4)),
            dma((4, 4, 2)), dma((4,)), dma((6,)), dma((6,)),
        ],
        compiler_params=pltpu.CompilerParams(
            collective_id=0, has_side_effects=True, vmem_limit_bytes=63 << 20
        ),
        cost_estimate=pl.CostEstimate(flops=3_300_000_000, bytes_accessed=8 << 20, transcendentals=2_200_000),
    )(q, k, v.reshape(4, BLK, GT), w, freq, doc_reset, rand_group, rand_slot, global_blocks)


def solution(mesh):
    placed = (
        P("ctx", "head"),
        P("ctx", "head"),
        P("ctx", "head"),
        P("head", None),
        P("ctx"),
        P("ctx", None),
        P("ctx", None),
        P(),
    )
    return jax.shard_map(
        on_device, mesh=mesh, in_specs=placed, out_specs=P(("ctx", "head"), None), check_vma=False
    )
```

```python
import math

import jax
import jax.numpy as jnp
import numpy as np
from jax import lax
from jax.experimental import pallas as pl
from jax.experimental.pallas import tpu as pltpu
from jax.sharding import PartitionSpec as P

HD = 128
BLK = 128
NZ, NX, NY = 8, 4, 4
GT = 512
WIDTH = 4096
TILE = 512
CHUNKS = (2, 1, 1)
ROPE_BASE = 500000.0
MESH = pl.DeviceIdType.MESH
F32 = jnp.float32
BF16 = jnp.bfloat16
SCORE_SCALE = HD ** (-0.5) * math.log2(math.e)


def sin_cos(angle):
    turns = jnp.floor(angle * (2.0 / math.pi) + 0.5)
    r = angle - turns * 1.5703125
    r = r - turns * 4.837512969970703125e-4
    r = r - turns * 7.54978995489188216e-8
    quarter = turns - 4.0 * jnp.floor(turns * 0.25)
    z = r * r
    s = r + r * z * (-1.6666654611e-1 + z * (8.3321608736e-3 + z * -1.9515295891e-4))
    c = 1.0 - 0.5 * z + z * z * (
        4.166664568298827e-2 + z * (-1.388731625493765e-3 + z * 2.443315711809948e-5)
    )
    odd = (quarter == 1.0) | (quarter == 3.0)
    sine = jnp.where(odd, c, s)
    cosine = jnp.where(odd, s, c)
    sine = jnp.where(quarter >= 2.0, -sine, sine)
    cosine = jnp.where((quarter == 1.0) | (quarter == 2.0), -cosine, cosine)
    return sine, cosine


def code(*digits):
    return sum(d * 4**k for k, d in enumerate(digits))


def kernel(
    q_hbm, k_hbm, v_hbm, w_hbm, freq_ref, doc_ref, group_ref, slot_ref, glob_ref, out_ref,
    meta_ref, qin, kin, qrot, krot, qbuf, kbuf, vbuf, wbuf, mall, meta_s, cos_t, sin_t,
    osend, obuf, st1, st2, st3, sa, sb, ra, rb, total,
    in_sem, w_sem, w_send, w_recv,
    mz_send, mz_recv, mx_send, mx_recv, ms_sem,
    z_send, z_recv, x_send, f_send, l_recv, r_recv, f_recv, s_send, s_recv,
    o_send, o_recv, y_send, y_recv,
):
    ctx = lax.axis_index("ctx")
    head = lax.axis_index("head")
    z, x = ctx // NX, ctx % NX
    y, c = head // 2, head % 2
    xr, xl = (x + 1) % NX, (x + NX - 1) % NX
    yr, yl = (y + 1) % NY, (y + NY - 1) % NY
    yo = (y + 2) % NY
    xo = (x + 2) % NX

    def dev(zz, xx, yy, cc):
        return (zz * NX + xx, yy * 2 + cc)

    sib = dev(z, x, y, 1 - c)

    def local(src, dst, sem):
        return pltpu.make_async_copy(src, dst, sem)

    def remote(src, dst, ssem, rsem, to):
        return pltpu.make_async_remote_copy(
            src_ref=src, dst_ref=dst, send_sem=ssem, recv_sem=rsem, device_id=to, device_id_type=MESH
        )

    def arrived(dst, sem):
        pltpu.make_async_copy(dst, dst, sem).wait()

    copy_k = local(k_hbm, kin, in_sem.at[0])
    copy_q = local(q_hbm, qin, in_sem.at[1])
    copy_k.start()
    copy_q.start()

    numbers = [doc_ref[b] for b in range(4)]
    numbers += [group_ref[b, n] * 4 + slot_ref[b, n] for b in range(4) for n in range(3)]
    spot = lax.broadcasted_iota(jnp.int32, (8, HD), 1)
    packed = jnp.zeros((8, HD), jnp.int32)
    for n, number in enumerate(numbers):
        packed = jnp.where(spot == n, number, packed)
    meta_ref[...] = packed

    barrier = pltpu.get_barrier_semaphore()
    for d in range(NZ):
        for e in range(2):
            if d or e:
                pl.semaphore_signal(
                    barrier, inc=1, device_id=dev((z + d) % NZ, x, y, (c + e) % 2), device_id_type=MESH
                )
    for xx in (xr, xl, xo):
        pl.semaphore_signal(barrier, inc=1, device_id=dev(z, xx, y, c), device_id_type=MESH)
    for yy in (yr, yl):
        pl.semaphore_signal(barrier, inc=1, device_id=dev(z, x, yy, c), device_id_type=MESH)
    pl.semaphore_wait(barrier, 2 * NZ - 1 + 3 + 2)

    meta_z = []
    for d in range(1, NZ):
        cp = remote(meta_ref, mall.at[x, z], mz_send.at[d - 1], mz_recv.at[d - 1], dev((z + d) % NZ, x, y, c))
        cp.start()
        meta_z.append(cp)
    mall[x, z] = meta_ref[...]

    def chunk(base, t, h):
        size = 4 // CHUNKS[t]
        return pl.ds(base * 4 + h * size, size)

    target_core = z % 2

    place = z % 4
    near = jnp.where(
        place == 0, code(0, 1, 2, 3),
        jnp.where(place == 1, code(1, 0, 2, 3), jnp.where(place == 2, code(2, 3, 1, 0), code(3, 2, 1, 0))),
    )
    far = jnp.where(
        place == 0, code(3, 2, 1, 0),
        jnp.where(place == 1, code(3, 2, 0, 1), jnp.where(place == 2, code(0, 1, 3, 2), code(0, 1, 2, 3))),
    )
    targets = jnp.where(z // 4 == c, near, far)
    target = [(targets // 4**k) % 4 for k in range(4)]
    nearest = (z - c + 1) // 2 + 4
    sender = [(nearest + d) % 4 for d in (0, 3, 1, 2)]

    def z_piece(t, h, j):
        if t == 0:
            src = v_hbm.at[chunk(0, t, h), :, pl.ds(pl.multiple_of(j * HD, HD), HD)]
            return src, vbuf.at[chunk(ctx, t, h)]
        if t == 1:
            return krot.at[j, chunk(0, t, h)], kbuf.at[chunk(ctx, t, h)]
        return qrot.at[j, chunk(0, t, h)], qbuf.at[chunk(z // 2, t, h)]

    def z_start(t, h, j):
        row = 4 * c + j
        same = (row == z) & (target_core == c)
        src, dst = z_piece(t, h, j)
        send, recv = z_send.at[t, h, j], z_recv.at[t, h, z // 2]

        @pl.when(same)
        def _():
            local(src, dst, recv).start()

        @pl.when(jnp.logical_not(same))
        def _():
            remote(src, dst, send, recv, dev(row, x, y, target_core)).start()

    def z_done(t, h, j):
        row = 4 * c + j
        same = (row == z) & (target_core == c)
        src, dst = z_piece(t, h, j)

        @pl.when(jnp.logical_not(same))
        def _():
            remote(src, dst, z_send.at[t, h, j], z_recv.at[t, h, z // 2], dev(row, x, y, target_core)).wait_send()

    bufs = (vbuf, kbuf)

    def group_from(i, xx):
        return (2 * i + c) * NX + xx

    def x_out(t, h, i, k, to_x, recv):
        piece = bufs[t].at[chunk(group_from(i, x), t, h)]
        return remote(piece, piece, x_send.at[t, h, i, k], recv.at[t, h, i], dev(z, to_x, y, c))

    def row_blocks(i, core):
        return pl.ds((2 * i + core) * 4 * NX, 4 * NX)

    def share(t, i):
        piece = bufs[t].at[row_blocks(i, c)]
        return remote(piece, piece, s_send.at[t, i], s_recv.at[t, i], sib)

    def forward(t, h, i):
        from_x = jnp.where(c == 0, xl, xr)
        to_x = jnp.where(c == 0, xr, xl)
        piece = bufs[t].at[chunk(group_from(i, from_x), t, h)]
        return remote(piece, piece, f_send.at[t, h, i], f_recv.at[t, h, i], dev(z, to_x, y, c))

    def own_step(t, h, n):
        i = sender[n]
        arrived(bufs[t].at[chunk(group_from(i, x), t, h)], z_recv.at[t, h, i])
        x_out(t, h, i, 0, xr, l_recv).start()
        x_out(t, h, i, 1, xl, r_recv).start()

    def side_step(t, h, n):
        i = sender[n]
        arrived(bufs[t].at[chunk(group_from(i, xl), t, h)], l_recv.at[t, h, i])

        @pl.when(c == 0)
        def _():
            forward(t, h, i).start()

        arrived(bufs[t].at[chunk(group_from(i, xr), t, h)], r_recv.at[t, h, i])

        @pl.when(c == 1)
        def _():
            forward(t, h, i).start()


    def far_step(t, h, n):
        i = sender[n]
        arrived(bufs[t].at[chunk(group_from(i, xo), t, h)], f_recv.at[t, h, i])
        if h == CHUNKS[t] - 1:
            share(t, i).start()

    def z_chunk(t, h):
        if h < CHUNKS[t]:
            for j in target:
                z_start(t, h, j)

    z_chunk(0, 0)

    for cp in meta_z:
        cp.wait_recv()
    meta_x = []
    for d in range(1, NX):
        cp = remote(mall.at[x], mall.at[x], mx_send.at[d - 1], mx_recv.at[d - 1], dev(z, (x + d) % NX, y, c))
        cp.start()
        meta_x.append(cp)
    copy_s = local(mall.at[x], meta_s, ms_sem)
    copy_s.start()
    for n in range(4):
        own_step(0, 0, n)
        if n == 0:
            z_chunk(0, 1)
    for cp in meta_x:
        cp.wait_recv()

    doc = mall[:, :, 0, :].astype(F32)
    group_ids = lax.broadcasted_iota(jnp.int32, (NX, NZ, HD), 1) * NX + lax.broadcasted_iota(
        jnp.int32, (NX, NZ, HD), 0
    )
    lane = lax.broadcasted_iota(jnp.int32, (NX, NZ, HD), 2)
    block_ids = group_ids * 4 + lane
    starts = jnp.where((lane < 4) & (doc < float(BLK)), block_ids.astype(F32) * float(BLK) + doc, 0.0)
    own_doc = meta_ref[0:1, :].astype(F32)
    offset = lax.broadcasted_iota(jnp.int32, (BLK, HD), 0).astype(F32)
    half_sign = jnp.where(lax.broadcasted_iota(jnp.int32, (BLK, HD), 1) < HD // 2, -1.0, 1.0)
    for b in range(4):
        block = ctx * 4 + b
        before = jnp.where(block_ids < block, starts, 0.0)
        before = jnp.max(jnp.max(before, axis=0), axis=0, keepdims=True)
        before = jnp.max(before, axis=1, keepdims=True)
        reset = own_doc[0:1, b : b + 1]
        first = (block * BLK).astype(F32)
        begin = jnp.where(offset >= reset, first + reset, before)
        angle = (first + offset - begin) * freq_ref[0:1, :]
        sine, cosine = sin_cos(angle)
        cos_t[b * BLK : (b + 1) * BLK, :] = cosine
        sin_t[b * BLK : (b + 1) * BLK, :] = sine * half_sign

    def rotate(src, dst, j):
        for b in range(4):
            rows = pl.ds(b * BLK, BLK)
            value = src[rows, j * HD : (j + 1) * HD].astype(F32)
            turned = value * cos_t[rows, :] + pltpu.roll(value, HD // 2, 1) * sin_t[rows, :]
            dst[j, b] = turned.astype(BF16)

    copy_k.wait()
    for j in range(4):
        rotate(kin, krot, j)
    z_chunk(1, 0)
    for h in range(1, CHUNKS[0]):
        for n in range(4):
            own_step(0, h, n)
            if n == 0:
                z_chunk(0, h + 1)
            side_step(0, h - 1, n)
        if h == 1:
            copy_q.wait()
            for j in range(4):
                rotate(qin, qrot, j)
    w_rows = pl.ds(pl.multiple_of(c * GT, GT), GT)
    w_other = pl.ds(pl.multiple_of((1 - c) * GT, GT), GT)
    copy_w = remote(w_hbm, wbuf.at[w_rows], w_send, w_recv, sib)
    copy_w.start()
    keep_w = local(w_hbm, wbuf.at[w_rows], w_sem)
    keep_w.start()

    last = CHUNKS[0] - 1
    for h in range(CHUNKS[1]):
        for n in range(4):
            own_step(1, h, n)
            if n == 0:
                z_chunk(1, h + 1)
            if h == 0:
                side_step(0, last, n)
            else:
                side_step(1, h - 1, n)
    z_chunk(2, 0)
    for h in range(CHUNKS[0]):
        for n in range(4):
            if h == 0:
                side_step(1, CHUNKS[1] - 1, n)
            far_step(0, h, n)
    for h in range(CHUNKS[1]):
        for n in range(4):
            far_step(1, h, n)

    def from_sibling(t):
        @pl.loop(0, 4)
        def _(i):
            arrived(bufs[t].at[row_blocks(i, 1 - c)], s_recv.at[t, i])

    from_sibling(0)
    from_sibling(1)

    @pl.loop(0, 4)
    def _(i):
        for h in range(CHUNKS[2]):
            arrived(qbuf.at[chunk(i, 2, h)], z_recv.at[2, h, i])

    copy_s.wait()

    ones = jnp.ones((8 * BLK, HD), BF16)
    order = (yo, yr, yl, y)

    def o_copies(step, b, i):
        zz = 2 * i + c
        for e in range(2):
            src = osend.at[step, i, pl.ds(e * 64, 64)]
            dst = obuf.at[b * NZ + z]
            yield e, (zz == z) & (c == e), src, dst, dev(zz, x, y, e)

    def attend(step):
        b = order[step]

        @pl.loop(0, 4, unroll=True)
        def _(i):
            zz = 2 * i + c
            block = (zz * NX + x) * 4 + b
            ids = [
                jnp.maximum(block - 1, 0),
                block,
                jnp.minimum(block + 1, 127),
                glob_ref[0],
                glob_ref[1],
                meta_s[zz, 0, 4 + b * 3],
                meta_s[zz, 0, 5 + b * 3],
                meta_s[zz, 0, 6 + b * 3],
            ]
            q = qbuf[i * 4 + b]
            keys = jnp.concatenate([kbuf[n] for n in ids], axis=0)
            scores = lax.dot_general(q, keys, (((1,), (1,)), ((), ())), preferred_element_type=F32)
            low = jnp.where(block > 0, 0.0, -1e30).astype(F32)
            high = jnp.where(block < 127, 0.0, -1e30).astype(F32)
            scores = jnp.concatenate(
                [
                    scores[:, :BLK] + low,
                    scores[:, BLK : 2 * BLK],
                    scores[:, 2 * BLK : 3 * BLK] + high,
                    scores[:, 3 * BLK :],
                ],
                axis=1,
            ) * SCORE_SCALE
            top = jnp.max(scores, axis=1, keepdims=True)
            weights = jnp.exp2(scores - top).astype(BF16)
            values = jnp.concatenate([vbuf[n] for n in ids], axis=0)
            both = jnp.dot(weights, jnp.concatenate([values, ones], axis=1), preferred_element_type=F32)
            osend[step, i] = (both[:, :HD] / both[:, HD:]).astype(BF16)
            for e, same, src, dst, to in o_copies(step, b, i):

                @pl.when(same)
                def _():
                    local(src, dst, o_recv.at[step]).start()

                @pl.when(jnp.logical_not(same))
                def _():
                    remote(src, dst, o_send.at[step, i, e], o_recv.at[step], to).start()

    def outputs_of(step):
        b = order[step]
        arrived(obuf.at[pl.ds(b * NZ, NZ)], o_recv.at[step])
        return b

    def project(b, first, last, finish):
        @pl.loop(first, last, unroll=True)
        def _(n):
            cols = pl.ds(pl.multiple_of(n * TILE, TILE), TILE)
            rows = jnp.concatenate([obuf[b * NZ + m] for m in range(NZ)], axis=1)
            finish(cols, jnp.dot(rows, wbuf[:, cols], preferred_element_type=F32))

    half = WIDTH // 2
    tiles = WIDTH // TILE
    left, right = pl.ds(0, half), pl.ds(half, half)

    def y_copy(k, src, dst, yy):
        return remote(src, dst, y_send.at[k], y_recv.at[k], dev(z, x, yy, c))

    y_copies = [
        y_copy(0, st1.at[:, left], sa, yr),
        y_copy(1, st1.at[:, right], sb, yl),
        y_copy(2, st2.at[:, right], ra.at[:, right], yr),
        y_copy(3, st2.at[:, left], ra.at[:, left], yr),
        y_copy(4, st3.at[:, left], rb.at[:, left], yl),
        y_copy(5, st3.at[:, right], rb.at[:, right], yl),
    ]

    def put(ref):
        def finish(cols, tile):
            ref[:, cols] = tile.astype(ref.dtype)

        return finish

    def project_0():
        b = outputs_of(0)
        project(b, 0, tiles // 2, put(st1))
        y_copies[0].start()
        project(b, tiles // 2, tiles, put(st1))
        y_copies[1].start()

    def project_1_near():
        b = outputs_of(1)
        project(b, tiles // 2, tiles, put(st2))

    def project_1_far():
        def finish(cols, tile):
            st2[:, cols] = (tile + sa[:, cols].astype(F32)).astype(BF16)

        y_copies[0].wait_recv()
        project(order[1], 0, tiles // 2, finish)
        y_copies[3].start()

    def project_2_near():
        b = outputs_of(2)
        project(b, 0, tiles // 2, put(st3))

    def project_2_far():
        y_copies[1].wait_recv()
        b = order[2]

        @pl.loop(tiles // 2, tiles, unroll=True)
        def _(n):
            cols = pl.ds(pl.multiple_of(n * TILE, TILE), TILE)
            near = pl.ds(pl.multiple_of(n * TILE - half, TILE), TILE)
            rows = jnp.concatenate([obuf[b * NZ + m] for m in range(NZ)], axis=1)
            tile = jnp.dot(rows, wbuf[:, cols], preferred_element_type=F32)
            st3[:, cols] = (tile + sb[:, near].astype(F32)).astype(BF16)

        y_copies[5].start()

    def project_3():
        b = outputs_of(3)
        project(b, 0, tiles, put(total))

    def first_phase_left():
        for cp in meta_z:
            cp.wait_send()
        for cp in meta_x:
            cp.wait_send()
        for j in range(4):
            for t in range(3):
                for h in range(CHUNKS[t]):
                    z_done(t, h, j)
        for t in range(2):

            @pl.loop(0, 4)
            def _(i):
                for h in range(CHUNKS[t]):
                    x_out(t, h, i, 0, xr, l_recv).wait_send()
                    x_out(t, h, i, 1, xl, r_recv).wait_send()
                    forward(t, h, i).wait_send()
                share(t, i).wait_send()

    attend(0)
    attend(1)
    keep_w.wait()
    copy_w.wait_send()
    arrived(wbuf.at[w_other], w_recv)
    attend(2)
    project_0()
    project_1_near()
    attend(3)
    first_phase_left()
    y_copies[0].wait_send()
    y_copies[2].start()
    project_2_near()
    y_copies[1].wait_send()
    y_copies[4].start()
    project_1_far()
    project_2_far()
    project_3()
    for k in (2, 3, 4, 5):
        y_copies[k].wait_recv()

    @pl.loop(0, tiles)
    def _(n):
        cols = pl.ds(pl.multiple_of(n * TILE, TILE), TILE)
        out_ref[:, cols] = (total[:, cols] + ra[:, cols].astype(F32) + rb[:, cols].astype(F32)).astype(BF16)

    for step in range(4):

        @pl.loop(0, 4)
        def _(i):
            for e, same, src, dst, to in o_copies(step, order[step], i):

                @pl.when(jnp.logical_not(same))
                def _():
                    remote(src, dst, o_send.at[step, i, e], o_recv.at[step], to).wait_send()

    for cp in y_copies[2:]:
        cp.wait_send()


def on_device(q, k, v, w, doc_reset, rand_group, rand_slot, global_blocks):
    pair = np.arange(HD // 2, dtype=np.float64) * (2.0 / HD)
    freq = np.exp(-pair * math.log(ROPE_BASE)).astype(np.float32)
    freq = jnp.asarray(np.broadcast_to(np.concatenate([freq, freq])[None], (8, HD)).copy())
    deep = max(CHUNKS)
    vmem = pltpu.VMEM
    dma = pltpu.SemaphoreType.DMA
    any_spec = pl.BlockSpec(memory_space=pl.ANY)
    vmem_spec = pl.BlockSpec(memory_space=pltpu.VMEM)
    return pl.pallas_call(
        kernel,
        out_shape=jax.ShapeDtypeStruct((64, WIDTH), BF16),
        in_specs=[any_spec] * 4 + [vmem_spec] + [pl.BlockSpec(memory_space=pltpu.SMEM)] * 4,
        out_specs=vmem_spec,
        scratch_shapes=[
            vmem((8, HD), jnp.int32),
            vmem((GT, GT), BF16),
            vmem((GT, GT), BF16),
            vmem((4, 4, BLK, HD), BF16),
            vmem((4, 4, BLK, HD), BF16),
            vmem((16, BLK, HD), BF16),
            vmem((128, BLK, HD), BF16),
            vmem((128, BLK, HD), BF16),
            vmem((2 * GT, WIDTH), BF16),
            vmem((NX, NZ, 8, HD), jnp.int32),
            pltpu.SMEM((NZ, 8, HD), jnp.int32),
            vmem((GT, HD), F32),
            vmem((GT, HD), F32),
            vmem((4, 4, BLK, HD), BF16),
            vmem((4 * NZ, 64, HD), BF16),
            vmem((64, WIDTH), BF16),
            vmem((64, WIDTH), BF16),
            vmem((64, WIDTH), BF16),
            vmem((64, WIDTH // 2), BF16),
            vmem((64, WIDTH // 2), BF16),
            vmem((64, WIDTH), BF16),
            vmem((64, WIDTH), BF16),
            vmem((64, WIDTH), F32),
            dma((2,)), dma, dma, dma,
            dma((NZ - 1,)), dma((NZ - 1,)), dma((NX - 1,)), dma((NX - 1,)), dma,
            dma((3, deep, 4)), dma((3, deep, 4)), dma((2, deep, 4, 2)), dma((2, deep, 4)),
            dma((2, deep, 4)), dma((2, deep, 4)), dma((2, deep, 4)), dma((2, 4)), dma((2, 4)),
            dma((4, 4, 2)), dma((4,)), dma((6,)), dma((6,)),
        ],
        compiler_params=pltpu.CompilerParams(
            collective_id=0, has_side_effects=True, vmem_limit_bytes=63 << 20
        ),
        cost_estimate=pl.CostEstimate(flops=3_300_000_000, bytes_accessed=8 << 20, transcendentals=2_200_000),
    )(q, k, v.reshape(4, BLK, GT), w, freq, doc_reset, rand_group, rand_slot, global_blocks)


def solution(mesh):
    placed = (
        P("ctx", "head"),
        P("ctx", "head"),
        P("ctx", "head"),
        P("head", None),
        P("ctx"),
        P("ctx", None),
        P("ctx", None),
        P(),
    )
    return jax.shard_map(
        on_device, mesh=mesh, in_specs=placed, out_specs=P(("ctx", "head"), None), check_vma=False
    )
```

```python
import math

import jax
import jax.numpy as jnp
import numpy as np
from jax import lax
from jax.experimental import pallas as pl
from jax.experimental.pallas import tpu as pltpu
from jax.sharding import PartitionSpec as P

HD = 128
BLK = 128
NZ, NX, NY = 8, 4, 4
GT = 512
WIDTH = 4096
TILE = 512
CHUNKS = (2, 1, 1)
ROPE_BASE = 500000.0
MESH = pl.DeviceIdType.MESH
F32 = jnp.float32
BF16 = jnp.bfloat16
SCORE_SCALE = HD ** (-0.5) * math.log2(math.e)


def sin_cos(angle):
    turns = jnp.floor(angle * (2.0 / math.pi) + 0.5)
    r = angle - turns * 1.5703125
    r = r - turns * 4.837512969970703125e-4
    r = r - turns * 7.54978995489188216e-8
    quarter = turns - 4.0 * jnp.floor(turns * 0.25)
    z = r * r
    s = r + r * z * (-1.6666654611e-1 + z * (8.3321608736e-3 + z * -1.9515295891e-4))
    c = 1.0 - 0.5 * z + z * z * (
        4.166664568298827e-2 + z * (-1.388731625493765e-3 + z * 2.443315711809948e-5)
    )
    odd = (quarter == 1.0) | (quarter == 3.0)
    sine = jnp.where(odd, c, s)
    cosine = jnp.where(odd, s, c)
    sine = jnp.where(quarter >= 2.0, -sine, sine)
    cosine = jnp.where((quarter == 1.0) | (quarter == 2.0), -cosine, cosine)
    return sine, cosine


def code(*digits):
    return sum(d * 4**k for k, d in enumerate(digits))


def kernel(
    q_hbm, k_hbm, v_hbm, w_hbm, freq_ref, doc_ref, group_ref, slot_ref, glob_ref, out_ref,
    meta_ref, qin, kin, qrot, krot, qbuf, kbuf, vbuf, wbuf, mall, meta_s, cos_t, sin_t,
    osend, obuf, st1, st2, st3, sa, sb, ra, rb, total,
    in_sem, w_sem, w_send, w_recv,
    mz_send, mz_recv, mx_send, mx_recv, ms_sem,
    z_send, z_recv, x_send, f_send, l_recv, r_recv, f_recv, s_send, s_recv,
    o_send, o_recv, y_send, y_recv,
):
    ctx = lax.axis_index("ctx")
    head = lax.axis_index("head")
    z, x = ctx // NX, ctx % NX
    y, c = head // 2, head % 2
    xr, xl = (x + 1) % NX, (x + NX - 1) % NX
    yr, yl = (y + 1) % NY, (y + NY - 1) % NY
    yo = (y + 2) % NY
    xo = (x + 2) % NX

    def dev(zz, xx, yy, cc):
        return (zz * NX + xx, yy * 2 + cc)

    sib = dev(z, x, y, 1 - c)

    def local(src, dst, sem):
        return pltpu.make_async_copy(src, dst, sem)

    def remote(src, dst, ssem, rsem, to):
        return pltpu.make_async_remote_copy(
            src_ref=src, dst_ref=dst, send_sem=ssem, recv_sem=rsem, device_id=to, device_id_type=MESH
        )

    def arrived(dst, sem):
        pltpu.make_async_copy(dst, dst, sem).wait()

    copy_k = local(k_hbm, kin, in_sem.at[0])
    copy_q = local(q_hbm, qin, in_sem.at[1])
    copy_k.start()
    copy_q.start()

    numbers = [doc_ref[b] for b in range(4)]
    numbers += [group_ref[b, n] * 4 + slot_ref[b, n] for b in range(4) for n in range(3)]
    spot = lax.broadcasted_iota(jnp.int32, (8, HD), 1)
    packed = jnp.zeros((8, HD), jnp.int32)
    for n, number in enumerate(numbers):
        packed = jnp.where(spot == n, number, packed)
    meta_ref[...] = packed

    barrier = pltpu.get_barrier_semaphore()
    for d in range(NZ):
        for e in range(2):
            if d or e:
                pl.semaphore_signal(
                    barrier, inc=1, device_id=dev((z + d) % NZ, x, y, (c + e) % 2), device_id_type=MESH
                )
    for xx in (xr, xl, xo):
        pl.semaphore_signal(barrier, inc=1, device_id=dev(z, xx, y, c), device_id_type=MESH)
    for yy in (yr, yl):
        pl.semaphore_signal(barrier, inc=1, device_id=dev(z, x, yy, c), device_id_type=MESH)
    pl.semaphore_wait(barrier, 2 * NZ - 1 + 3 + 2)

    meta_z = []
    for d in range(1, NZ):
        cp = remote(meta_ref, mall.at[x, z], mz_send.at[d - 1], mz_recv.at[d - 1], dev((z + d) % NZ, x, y, c))
        cp.start()
        meta_z.append(cp)
    mall[x, z] = meta_ref[...]

    def chunk(base, t, h):
        size = 4 // CHUNKS[t]
        return pl.ds(base * 4 + h * size, size)

    target_core = z % 2

    place = z % 4
    near = jnp.where(
        place == 0, code(0, 1, 2, 3),
        jnp.where(place == 1, code(1, 0, 2, 3), jnp.where(place == 2, code(2, 3, 1, 0), code(3, 2, 1, 0))),
    )
    far = jnp.where(
        place == 0, code(3, 2, 1, 0),
        jnp.where(place == 1, code(3, 2, 0, 1), jnp.where(place == 2, code(0, 1, 3, 2), code(0, 1, 2, 3))),
    )
    targets = jnp.where(z // 4 == c, near, far)
    target = [(targets // 4**k) % 4 for k in range(4)]
    nearest = (z - c + 1) // 2 + 4
    sender = [(nearest + d) % 4 for d in (0, 3, 1, 2)]

    def z_piece(t, h, j):
        if t == 0:
            src = v_hbm.at[chunk(0, t, h), :, pl.ds(pl.multiple_of(j * HD, HD), HD)]
            return src, vbuf.at[chunk(ctx, t, h)]
        if t == 1:
            return krot.at[j, chunk(0, t, h)], kbuf.at[chunk(ctx, t, h)]
        return qrot.at[j, chunk(0, t, h)], qbuf.at[chunk(z // 2, t, h)]

    def z_start(t, h, j):
        row = 4 * c + j
        same = (row == z) & (target_core == c)
        src, dst = z_piece(t, h, j)
        send, recv = z_send.at[t, h, j], z_recv.at[t, h, z // 2]

        @pl.when(same)
        def _():
            local(src, dst, recv).start()

        @pl.when(jnp.logical_not(same))
        def _():
            remote(src, dst, send, recv, dev(row, x, y, target_core)).start()

    def z_done(t, h, j):
        row = 4 * c + j
        same = (row == z) & (target_core == c)
        src, dst = z_piece(t, h, j)

        @pl.when(jnp.logical_not(same))
        def _():
            remote(src, dst, z_send.at[t, h, j], z_recv.at[t, h, z // 2], dev(row, x, y, target_core)).wait_send()

    bufs = (vbuf, kbuf)

    def group_from(i, xx):
        return (2 * i + c) * NX + xx

    def x_out(t, h, i, k, to_x, recv):
        piece = bufs[t].at[chunk(group_from(i, x), t, h)]
        return remote(piece, piece, x_send.at[t, h, i, k], recv.at[t, h, i], dev(z, to_x, y, c))

    def row_blocks(i, core):
        return pl.ds((2 * i + core) * 4 * NX, 4 * NX)

    def share(t, i):
        piece = bufs[t].at[row_blocks(i, c)]
        return remote(piece, piece, s_send.at[t, i], s_recv.at[t, i], sib)

    def forward(t, h, i):
        from_x = jnp.where(c == 0, xl, xr)
        to_x = jnp.where(c == 0, xr, xl)
        piece = bufs[t].at[chunk(group_from(i, from_x), t, h)]
        return remote(piece, piece, f_send.at[t, h, i], f_recv.at[t, h, i], dev(z, to_x, y, c))

    def own_step(t, h, n):
        i = sender[n]
        arrived(bufs[t].at[chunk(group_from(i, x), t, h)], z_recv.at[t, h, i])
        x_out(t, h, i, 0, xr, l_recv).start()
        x_out(t, h, i, 1, xl, r_recv).start()

    def side_step(t, h, n):
        i = sender[n]
        arrived(bufs[t].at[chunk(group_from(i, xl), t, h)], l_recv.at[t, h, i])

        @pl.when(c == 0)
        def _():
            forward(t, h, i).start()

        arrived(bufs[t].at[chunk(group_from(i, xr), t, h)], r_recv.at[t, h, i])

        @pl.when(c == 1)
        def _():
            forward(t, h, i).start()


    def far_step(t, h, n):
        i = sender[n]
        arrived(bufs[t].at[chunk(group_from(i, xo), t, h)], f_recv.at[t, h, i])
        if h == CHUNKS[t] - 1:
            share(t, i).start()

    def z_chunk(t, h):
        if h < CHUNKS[t]:
            for j in target:
                z_start(t, h, j)

    z_chunk(0, 0)

    for cp in meta_z:
        cp.wait_recv()
    meta_x = []
    for d in range(1, NX):
        cp = remote(mall.at[x], mall.at[x], mx_send.at[d - 1], mx_recv.at[d - 1], dev(z, (x + d) % NX, y, c))
        cp.start()
        meta_x.append(cp)
    copy_s = local(mall.at[x], meta_s, ms_sem)
    copy_s.start()
    for n in range(4):
        own_step(0, 0, n)
        if n == 0:
            z_chunk(0, 1)
    for cp in meta_x:
        cp.wait_recv()

    doc = mall[:, :, 0, :].astype(F32)
    group_ids = lax.broadcasted_iota(jnp.int32, (NX, NZ, HD), 1) * NX + lax.broadcasted_iota(
        jnp.int32, (NX, NZ, HD), 0
    )
    lane = lax.broadcasted_iota(jnp.int32, (NX, NZ, HD), 2)
    block_ids = group_ids * 4 + lane
    starts = jnp.where((lane < 4) & (doc < float(BLK)), block_ids.astype(F32) * float(BLK) + doc, 0.0)
    own_doc = meta_ref[0:1, :].astype(F32)
    offset = lax.broadcasted_iota(jnp.int32, (BLK, HD), 0).astype(F32)
    half_sign = jnp.where(lax.broadcasted_iota(jnp.int32, (BLK, HD), 1) < HD // 2, -1.0, 1.0)
    for b in range(4):
        block = ctx * 4 + b
        before = jnp.where(block_ids < block, starts, 0.0)
        before = jnp.max(jnp.max(before, axis=0), axis=0, keepdims=True)
        before = jnp.max(before, axis=1, keepdims=True)
        reset = own_doc[0:1, b : b + 1]
        first = (block * BLK).astype(F32)
        begin = jnp.where(offset >= reset, first + reset, before)
        angle = (first + offset - begin) * freq_ref[0:1, :]
        sine, cosine = sin_cos(angle)
        cos_t[b * BLK : (b + 1) * BLK, :] = cosine
        sin_t[b * BLK : (b + 1) * BLK, :] = sine * half_sign

    def rotate(src, dst, j):
        for b in range(4):
            rows = pl.ds(b * BLK, BLK)
            value = src[rows, j * HD : (j + 1) * HD].astype(F32)
            turned = value * cos_t[rows, :] + pltpu.roll(value, HD // 2, 1) * sin_t[rows, :]
            dst[j, b] = turned.astype(BF16)

    copy_k.wait()
    for j in range(4):
        rotate(kin, krot, j)
    z_chunk(1, 0)
    for h in range(1, CHUNKS[0]):
        for n in range(4):
            own_step(0, h, n)
            if n == 0:
                z_chunk(0, h + 1)
            side_step(0, h - 1, n)
        if h == 1:
            copy_q.wait()
            for j in range(4):
                rotate(qin, qrot, j)
    w_rows = pl.ds(pl.multiple_of(c * GT, GT), GT)
    w_other = pl.ds(pl.multiple_of((1 - c) * GT, GT), GT)
    copy_w = remote(w_hbm, wbuf.at[w_rows], w_send, w_recv, sib)
    copy_w.start()
    keep_w = local(w_hbm, wbuf.at[w_rows], w_sem)
    keep_w.start()

    last = CHUNKS[0] - 1
    for h in range(CHUNKS[1]):
        for n in range(4):
            own_step(1, h, n)
            if n == 0:
                z_chunk(1, h + 1)
            if h == 0:
                side_step(0, last, n)
            else:
                side_step(1, h - 1, n)
    z_chunk(2, 0)
    for h in range(CHUNKS[0]):
        for n in range(4):
            if h == 0:
                side_step(1, CHUNKS[1] - 1, n)
            far_step(0, h, n)
    for h in range(CHUNKS[1]):
        for n in range(4):
            far_step(1, h, n)

    def from_sibling(t):
        @pl.loop(0, 4)
        def _(i):
            arrived(bufs[t].at[row_blocks(i, 1 - c)], s_recv.at[t, i])

    from_sibling(0)
    from_sibling(1)

    @pl.loop(0, 4)
    def _(i):
        for h in range(CHUNKS[2]):
            arrived(qbuf.at[chunk(i, 2, h)], z_recv.at[2, h, i])

    copy_s.wait()

    ones = jnp.ones((8 * BLK, HD), BF16)
    order = (yo, yr, yl, y)

    def o_copies(step, b, i):
        zz = 2 * i + c
        for e in range(2):
            src = osend.at[step, i, pl.ds(e * 64, 64)]
            dst = obuf.at[b * NZ + z]
            yield e, (zz == z) & (c == e), src, dst, dev(zz, x, y, e)

    def attend(step):
        b = order[step]

        @pl.loop(0, 4, unroll=True)
        def _(i):
            zz = 2 * i + c
            block = (zz * NX + x) * 4 + b
            ids = [
                jnp.maximum(block - 1, 0),
                block,
                jnp.minimum(block + 1, 127),
                glob_ref[0],
                glob_ref[1],
                meta_s[zz, 0, 4 + b * 3],
                meta_s[zz, 0, 5 + b * 3],
                meta_s[zz, 0, 6 + b * 3],
            ]
            q = qbuf[i * 4 + b]
            keys = jnp.concatenate([kbuf[n] for n in ids], axis=0)
            scores = lax.dot_general(q, keys, (((1,), (1,)), ((), ())), preferred_element_type=F32)
            low = jnp.where(block > 0, 0.0, -1e30).astype(F32)
            high = jnp.where(block < 127, 0.0, -1e30).astype(F32)
            scores = jnp.concatenate(
                [
                    scores[:, :BLK] + low,
                    scores[:, BLK : 2 * BLK],
                    scores[:, 2 * BLK : 3 * BLK] + high,
                    scores[:, 3 * BLK :],
                ],
                axis=1,
            ) * SCORE_SCALE
            top = jnp.max(scores, axis=1, keepdims=True)
            weights = jnp.exp2(scores - top).astype(BF16)
            values = jnp.concatenate([vbuf[n] for n in ids], axis=0)
            both = jnp.dot(weights, jnp.concatenate([values, ones], axis=1), preferred_element_type=F32)
            osend[step, i] = (both[:, :HD] / both[:, HD:]).astype(BF16)
            for e, same, src, dst, to in o_copies(step, b, i):

                @pl.when(same)
                def _():
                    local(src, dst, o_recv.at[step]).start()

                @pl.when(jnp.logical_not(same))
                def _():
                    remote(src, dst, o_send.at[step, i, e], o_recv.at[step], to).start()

    def outputs_of(step):
        b = order[step]
        arrived(obuf.at[pl.ds(b * NZ, NZ)], o_recv.at[step])
        return b

    def project(b, first, last, finish):
        @pl.loop(first, last, unroll=True)
        def _(n):
            cols = pl.ds(pl.multiple_of(n * TILE, TILE), TILE)
            rows = jnp.concatenate([obuf[b * NZ + m] for m in range(NZ)], axis=1)
            finish(cols, jnp.dot(rows, wbuf[:, cols], preferred_element_type=F32))

    half = WIDTH // 2
    tiles = WIDTH // TILE
    left, right = pl.ds(0, half), pl.ds(half, half)

    def y_copy(k, src, dst, yy):
        return remote(src, dst, y_send.at[k], y_recv.at[k], dev(z, x, yy, c))

    y_copies = [
        y_copy(0, st1.at[:, left], sa, yr),
        y_copy(1, st1.at[:, right], sb, yl),
        y_copy(2, st2.at[:, right], ra.at[:, right], yr),
        y_copy(3, st2.at[:, left], ra.at[:, left], yr),
        y_copy(4, st3.at[:, left], rb.at[:, left], yl),
        y_copy(5, st3.at[:, right], rb.at[:, right], yl),
    ]

    def put(ref):
        def finish(cols, tile):
            ref[:, cols] = tile.astype(ref.dtype)

        return finish

    def project_0():
        b = outputs_of(0)
        project(b, 0, tiles // 2, put(st1))
        y_copies[0].start()
        project(b, tiles // 2, tiles, put(st1))
        y_copies[1].start()

    def project_1_near():
        b = outputs_of(1)
        project(b, tiles // 2, tiles, put(st2))

    def project_1_far():
        def finish(cols, tile):
            st2[:, cols] = (tile + sa[:, cols].astype(F32)).astype(BF16)

        y_copies[0].wait_recv()
        project(order[1], 0, tiles // 2, finish)
        y_copies[3].start()

    def project_2_near():
        b = outputs_of(2)
        project(b, 0, tiles // 2, put(st3))

    def project_2_far():
        y_copies[1].wait_recv()
        b = order[2]

        @pl.loop(tiles // 2, tiles, unroll=True)
        def _(n):
            cols = pl.ds(pl.multiple_of(n * TILE, TILE), TILE)
            near = pl.ds(pl.multiple_of(n * TILE - half, TILE), TILE)
            rows = jnp.concatenate([obuf[b * NZ + m] for m in range(NZ)], axis=1)
            tile = jnp.dot(rows, wbuf[:, cols], preferred_element_type=F32)
            st3[:, cols] = (tile + sb[:, near].astype(F32)).astype(BF16)

        y_copies[5].start()

    def project_3():
        b = outputs_of(3)
        project(b, 0, tiles, put(total))

    def first_phase_left():
        for cp in meta_z:
            cp.wait_send()
        for cp in meta_x:
            cp.wait_send()
        for j in range(4):
            for t in range(3):
                for h in range(CHUNKS[t]):
                    z_done(t, h, j)
        for t in range(2):

            @pl.loop(0, 4)
            def _(i):
                for h in range(CHUNKS[t]):
                    x_out(t, h, i, 0, xr, l_recv).wait_send()
                    x_out(t, h, i, 1, xl, r_recv).wait_send()
                    forward(t, h, i).wait_send()
                share(t, i).wait_send()

    attend(0)
    attend(1)
    keep_w.wait()
    copy_w.wait_send()
    arrived(wbuf.at[w_other], w_recv)
    attend(2)
    project_0()
    project_1_near()
    attend(3)
    first_phase_left()
    y_copies[0].wait_send()
    y_copies[2].start()
    project_2_near()
    y_copies[1].wait_send()
    y_copies[4].start()
    project_1_far()
    project_2_far()
    project_3()
    def add_up(first):
        for n in range(first, first + tiles // 2):
            cols = pl.ds(n * TILE, TILE)
            total[:, cols] = total[:, cols] + (ra if first else rb)[:, cols].astype(F32)

    def finish_half(first):
        for n in range(first, first + tiles // 2):
            cols = pl.ds(n * TILE, TILE)
            out_ref[:, cols] = (total[:, cols] + (rb if first else ra)[:, cols].astype(F32)).astype(BF16)

    for step in range(4):

        @pl.loop(0, 4)
        def _(i):
            for e, same, src, dst, to in o_copies(step, order[step], i):

                @pl.when(jnp.logical_not(same))
                def _():
                    remote(src, dst, o_send.at[step, i, e], o_recv.at[step], to).wait_send()

    y_copies[2].wait_recv()
    add_up(tiles // 2)
    y_copies[4].wait_recv()
    add_up(0)
    y_copies[3].wait_recv()
    finish_half(0)
    y_copies[5].wait_recv()
    finish_half(tiles // 2)

    for cp in y_copies[2:]:
        cp.wait_send()


def on_device(q, k, v, w, doc_reset, rand_group, rand_slot, global_blocks):
    pair = np.arange(HD // 2, dtype=np.float64) * (2.0 / HD)
    freq = np.exp(-pair * math.log(ROPE_BASE)).astype(np.float32)
    freq = jnp.asarray(np.broadcast_to(np.concatenate([freq, freq])[None], (8, HD)).copy())
    deep = max(CHUNKS)
    vmem = pltpu.VMEM
    dma = pltpu.SemaphoreType.DMA
    any_spec = pl.BlockSpec(memory_space=pl.ANY)
    vmem_spec = pl.BlockSpec(memory_space=pltpu.VMEM)
    return pl.pallas_call(
        kernel,
        out_shape=jax.ShapeDtypeStruct((64, WIDTH), BF16),
        in_specs=[any_spec] * 4 + [vmem_spec] + [pl.BlockSpec(memory_space=pltpu.SMEM)] * 4,
        out_specs=vmem_spec,
        scratch_shapes=[
            vmem((8, HD), jnp.int32),
            vmem((GT, GT), BF16),
            vmem((GT, GT), BF16),
            vmem((4, 4, BLK, HD), BF16),
            vmem((4, 4, BLK, HD), BF16),
            vmem((16, BLK, HD), BF16),
            vmem((128, BLK, HD), BF16),
            vmem((128, BLK, HD), BF16),
            vmem((2 * GT, WIDTH), BF16),
            vmem((NX, NZ, 8, HD), jnp.int32),
            pltpu.SMEM((NZ, 8, HD), jnp.int32),
            vmem((GT, HD), F32),
            vmem((GT, HD), F32),
            vmem((4, 4, BLK, HD), BF16),
            vmem((4 * NZ, 64, HD), BF16),
            vmem((64, WIDTH), BF16),
            vmem((64, WIDTH), BF16),
            vmem((64, WIDTH), BF16),
            vmem((64, WIDTH // 2), BF16),
            vmem((64, WIDTH // 2), BF16),
            vmem((64, WIDTH), BF16),
            vmem((64, WIDTH), BF16),
            vmem((64, WIDTH), F32),
            dma((2,)), dma, dma, dma,
            dma((NZ - 1,)), dma((NZ - 1,)), dma((NX - 1,)), dma((NX - 1,)), dma,
            dma((3, deep, 4)), dma((3, deep, 4)), dma((2, deep, 4, 2)), dma((2, deep, 4)),
            dma((2, deep, 4)), dma((2, deep, 4)), dma((2, deep, 4)), dma((2, 4)), dma((2, 4)),
            dma((4, 4, 2)), dma((4,)), dma((6,)), dma((6,)),
        ],
        compiler_params=pltpu.CompilerParams(
            collective_id=0, has_side_effects=True, vmem_limit_bytes=63 << 20
        ),
        cost_estimate=pl.CostEstimate(flops=3_300_000_000, bytes_accessed=8 << 20, transcendentals=2_200_000),
    )(q, k, v.reshape(4, BLK, GT), w, freq, doc_reset, rand_group, rand_slot, global_blocks)


def solution(mesh):
    placed = (
        P("ctx", "head"),
        P("ctx", "head"),
        P("ctx", "head"),
        P("head", None),
        P("ctx"),
        P("ctx", None),
        P("ctx", None),
        P(),
    )
    return jax.shard_map(
        on_device, mesh=mesh, in_specs=placed, out_specs=P(("ctx", "head"), None), check_vma=False
    )
```

```python
import math

import jax
import jax.numpy as jnp
import numpy as np
from jax import lax
from jax.experimental import pallas as pl
from jax.experimental.pallas import tpu as pltpu
from jax.sharding import PartitionSpec as P

HD = 128
BLK = 128
NZ, NX, NY = 8, 4, 4
GT = 512
WIDTH = 4096
TILE = 512
CHUNKS = (2, 1, 1)
ROPE_BASE = 500000.0
MESH = pl.DeviceIdType.MESH
F32 = jnp.float32
BF16 = jnp.bfloat16
SCORE_SCALE = HD ** (-0.5) * math.log2(math.e)


def sin_cos(angle):
    turns = jnp.floor(angle * (2.0 / math.pi) + 0.5)
    r = angle - turns * 1.5703125
    r = r - turns * 4.837512969970703125e-4
    r = r - turns * 7.54978995489188216e-8
    quarter = turns - 4.0 * jnp.floor(turns * 0.25)
    z = r * r
    s = r + r * z * (-1.6666654611e-1 + z * (8.3321608736e-3 + z * -1.9515295891e-4))
    c = 1.0 - 0.5 * z + z * z * (
        4.166664568298827e-2 + z * (-1.388731625493765e-3 + z * 2.443315711809948e-5)
    )
    odd = (quarter == 1.0) | (quarter == 3.0)
    sine = jnp.where(odd, c, s)
    cosine = jnp.where(odd, s, c)
    sine = jnp.where(quarter >= 2.0, -sine, sine)
    cosine = jnp.where((quarter == 1.0) | (quarter == 2.0), -cosine, cosine)
    return sine, cosine


def code(*digits):
    return sum(d * 4**k for k, d in enumerate(digits))


def kernel(
    q_hbm, k_hbm, v_hbm, w_hbm, freq_ref, doc_ref, group_ref, slot_ref, glob_ref, out_ref,
    meta_ref, qin, kin, qrot, krot, qbuf, kbuf, vbuf, wbuf, mall, meta_s, cos_t, sin_t,
    osend, obuf, st1, st2, st3, sa, sb, ra, rb, total,
    in_sem, w_sem, w_send, w_recv,
    mz_send, mz_recv, mx_send, mx_recv, ms_sem,
    z_send, z_recv, x_send, f_send, l_recv, r_recv, f_recv, s_send, s_recv,
    o_send, o_recv, y_send, y_recv,
):
    ctx = lax.axis_index("ctx")
    head = lax.axis_index("head")
    z, x = ctx // NX, ctx % NX
    y, c = head // 2, head % 2
    xr, xl = (x + 1) % NX, (x + NX - 1) % NX
    yr, yl = (y + 1) % NY, (y + NY - 1) % NY
    yo = (y + 2) % NY
    xo = (x + 2) % NX

    def dev(zz, xx, yy, cc):
        return (zz * NX + xx, yy * 2 + cc)

    sib = dev(z, x, y, 1 - c)

    def local(src, dst, sem):
        return pltpu.make_async_copy(src, dst, sem)

    def remote(src, dst, ssem, rsem, to):
        return pltpu.make_async_remote_copy(
            src_ref=src, dst_ref=dst, send_sem=ssem, recv_sem=rsem, device_id=to, device_id_type=MESH
        )

    def arrived(dst, sem):
        pltpu.make_async_copy(dst, dst, sem).wait()

    copy_k = local(k_hbm, kin, in_sem.at[0])
    copy_q = local(q_hbm, qin, in_sem.at[1])
    copy_k.start()
    copy_q.start()

    numbers = [doc_ref[b] for b in range(4)]
    numbers += [group_ref[b, n] * 4 + slot_ref[b, n] for b in range(4) for n in range(3)]
    spot = lax.broadcasted_iota(jnp.int32, (8, HD), 1)
    packed = jnp.zeros((8, HD), jnp.int32)
    for n, number in enumerate(numbers):
        packed = jnp.where(spot == n, number, packed)
    meta_ref[...] = packed

    barrier = pltpu.get_barrier_semaphore()
    for d in range(NZ):
        for e in range(2):
            if d or e:
                pl.semaphore_signal(
                    barrier, inc=1, device_id=dev((z + d) % NZ, x, y, (c + e) % 2), device_id_type=MESH
                )
    for xx in (xr, xl, xo):
        pl.semaphore_signal(barrier, inc=1, device_id=dev(z, xx, y, c), device_id_type=MESH)
    for yy in (yr, yl):
        pl.semaphore_signal(barrier, inc=1, device_id=dev(z, x, yy, c), device_id_type=MESH)
    pl.semaphore_wait(barrier, 2 * NZ - 1 + 3 + 2)

    meta_z = []
    for d in range(1, NZ):
        cp = remote(meta_ref, mall.at[x, z], mz_send.at[d - 1], mz_recv.at[d - 1], dev((z + d) % NZ, x, y, c))
        cp.start()
        meta_z.append(cp)
    mall[x, z] = meta_ref[...]

    def chunk(base, t, h):
        size = 4 // CHUNKS[t]
        return pl.ds(base * 4 + h * size, size)

    target_core = z % 2

    place = z % 4
    near = jnp.where(
        place == 0, code(0, 1, 2, 3),
        jnp.where(place == 1, code(1, 0, 2, 3), jnp.where(place == 2, code(2, 3, 1, 0), code(3, 2, 1, 0))),
    )
    far = jnp.where(
        place == 0, code(3, 2, 1, 0),
        jnp.where(place == 1, code(3, 2, 0, 1), jnp.where(place == 2, code(0, 1, 3, 2), code(0, 1, 2, 3))),
    )
    targets = jnp.where(z // 4 == c, near, far)
    target = [(targets // 4**k) % 4 for k in range(4)]
    nearest = (z - c + 1) // 2 + 4
    sender = [(nearest + d) % 4 for d in (0, 3, 1, 2)]

    def z_piece(t, h, j):
        if t == 0:
            src = v_hbm.at[chunk(0, t, h), :, pl.ds(pl.multiple_of(j * HD, HD), HD)]
            return src, vbuf.at[chunk(ctx, t, h)]
        if t == 1:
            return krot.at[j, chunk(0, t, h)], kbuf.at[chunk(ctx, t, h)]
        return qrot.at[j, chunk(0, t, h)], qbuf.at[chunk(z // 2, t, h)]

    def z_start(t, h, j):
        row = 4 * c + j
        same = (row == z) & (target_core == c)
        src, dst = z_piece(t, h, j)
        send, recv = z_send.at[t, h, j], z_recv.at[t, h, z // 2]

        @pl.when(same)
        def _():
            local(src, dst, recv).start()

        @pl.when(jnp.logical_not(same))
        def _():
            remote(src, dst, send, recv, dev(row, x, y, target_core)).start()

    def z_done(t, h, j):
        row = 4 * c + j
        same = (row == z) & (target_core == c)
        src, dst = z_piece(t, h, j)

        @pl.when(jnp.logical_not(same))
        def _():
            remote(src, dst, z_send.at[t, h, j], z_recv.at[t, h, z // 2], dev(row, x, y, target_core)).wait_send()

    bufs = (vbuf, kbuf)

    def group_from(i, xx):
        return (2 * i + c) * NX + xx

    def x_out(t, h, i, k, to_x, recv):
        piece = bufs[t].at[chunk(group_from(i, x), t, h)]
        return remote(piece, piece, x_send.at[t, h, i, k], recv.at[t, h, i], dev(z, to_x, y, c))

    def row_blocks(i, core):
        return pl.ds((2 * i + core) * 4 * NX, 4 * NX)

    def share(t, i):
        piece = bufs[t].at[row_blocks(i, c)]
        return remote(piece, piece, s_send.at[t, i], s_recv.at[t, i], sib)

    def forward(t, h, i):
        from_x = jnp.where(c == 0, xl, xr)
        to_x = jnp.where(c == 0, xr, xl)
        piece = bufs[t].at[chunk(group_from(i, from_x), t, h)]
        return remote(piece, piece, f_send.at[t, h, i], f_recv.at[t, h, i], dev(z, to_x, y, c))

    def own_step(t, h, n):
        i = sender[n]
        arrived(bufs[t].at[chunk(group_from(i, x), t, h)], z_recv.at[t, h, i])
        x_out(t, h, i, 0, xr, l_recv).start()
        x_out(t, h, i, 1, xl, r_recv).start()

    def side_step(t, h, n):
        i = sender[n]
        arrived(bufs[t].at[chunk(group_from(i, xl), t, h)], l_recv.at[t, h, i])

        @pl.when(c == 0)
        def _():
            forward(t, h, i).start()

        arrived(bufs[t].at[chunk(group_from(i, xr), t, h)], r_recv.at[t, h, i])

        @pl.when(c == 1)
        def _():
            forward(t, h, i).start()


    def far_step(t, h, n):
        i = sender[n]
        arrived(bufs[t].at[chunk(group_from(i, xo), t, h)], f_recv.at[t, h, i])
        if h == CHUNKS[t] - 1:
            share(t, i).start()

    def z_chunk(t, h):
        if h < CHUNKS[t]:
            for j in target:
                z_start(t, h, j)

    z_chunk(0, 0)

    for cp in meta_z:
        cp.wait_recv()
    meta_x = []
    for d in range(1, NX):
        cp = remote(mall.at[x], mall.at[x], mx_send.at[d - 1], mx_recv.at[d - 1], dev(z, (x + d) % NX, y, c))
        cp.start()
        meta_x.append(cp)
    copy_s = local(mall.at[x], meta_s, ms_sem)
    copy_s.start()
    for n in range(4):
        own_step(0, 0, n)
        if n == 0:
            z_chunk(0, 1)
    for cp in meta_x:
        cp.wait_recv()

    doc = mall[:, :, 0, :].astype(F32)
    group_ids = lax.broadcasted_iota(jnp.int32, (NX, NZ, HD), 1) * NX + lax.broadcasted_iota(
        jnp.int32, (NX, NZ, HD), 0
    )
    lane = lax.broadcasted_iota(jnp.int32, (NX, NZ, HD), 2)
    block_ids = group_ids * 4 + lane
    starts = jnp.where((lane < 4) & (doc < float(BLK)), block_ids.astype(F32) * float(BLK) + doc, 0.0)
    own_doc = meta_ref[0:1, :].astype(F32)
    offset = lax.broadcasted_iota(jnp.int32, (BLK, HD), 0).astype(F32)
    half_sign = jnp.where(lax.broadcasted_iota(jnp.int32, (BLK, HD), 1) < HD // 2, -1.0, 1.0)
    for b in range(4):
        block = ctx * 4 + b
        before = jnp.where(block_ids < block, starts, 0.0)
        before = jnp.max(jnp.max(before, axis=0), axis=0, keepdims=True)
        before = jnp.max(before, axis=1, keepdims=True)
        reset = own_doc[0:1, b : b + 1]
        first = (block * BLK).astype(F32)
        begin = jnp.where(offset >= reset, first + reset, before)
        angle = (first + offset - begin) * freq_ref[0:1, :]
        sine, cosine = sin_cos(angle)
        cos_t[b * BLK : (b + 1) * BLK, :] = cosine
        sin_t[b * BLK : (b + 1) * BLK, :] = sine * half_sign

    def rotate(src, dst, j):
        for b in range(4):
            rows = pl.ds(b * BLK, BLK)
            value = src[rows, j * HD : (j + 1) * HD].astype(F32)
            turned = value * cos_t[rows, :] + pltpu.roll(value, HD // 2, 1) * sin_t[rows, :]
            dst[j, b] = turned.astype(BF16)

    copy_k.wait()
    for j in range(4):
        rotate(kin, krot, j)
    z_chunk(1, 0)
    for h in range(1, CHUNKS[0]):
        for n in range(4):
            own_step(0, h, n)
            if n == 0:
                z_chunk(0, h + 1)
            side_step(0, h - 1, n)
        if h == 1:
            copy_q.wait()
            for j in range(4):
                rotate(qin, qrot, j)
    w_rows = pl.ds(pl.multiple_of(c * GT, GT), GT)
    w_other = pl.ds(pl.multiple_of((1 - c) * GT, GT), GT)
    copy_w = remote(w_hbm, wbuf.at[w_rows], w_send, w_recv, sib)
    copy_w.start()
    keep_w = local(w_hbm, wbuf.at[w_rows], w_sem)
    keep_w.start()

    last = CHUNKS[0] - 1
    for h in range(CHUNKS[1]):
        for n in range(4):
            own_step(1, h, n)
            if n == 0:
                z_chunk(1, h + 1)
            if h == 0:
                side_step(0, last, n)
            else:
                side_step(1, h - 1, n)
    z_chunk(2, 0)
    for h in range(CHUNKS[0]):
        for n in range(4):
            if h == 0:
                side_step(1, CHUNKS[1] - 1, n)
            far_step(0, h, n)
    for h in range(CHUNKS[1]):
        for n in range(4):
            far_step(1, h, n)

    def from_sibling(t):
        @pl.loop(0, 4)
        def _(i):
            arrived(bufs[t].at[row_blocks(i, 1 - c)], s_recv.at[t, i])

    from_sibling(0)
    from_sibling(1)

    @pl.loop(0, 4)
    def _(i):
        for h in range(CHUNKS[2]):
            arrived(qbuf.at[chunk(i, 2, h)], z_recv.at[2, h, i])

    copy_s.wait()

    ones = jnp.ones((8 * BLK, HD), BF16)
    order = (yo, yr, yl, y)

    def o_copies(step, b, i):
        zz = 2 * i + c
        for e in range(2):
            src = osend.at[step, i, pl.ds(e * 64, 64)]
            dst = obuf.at[b * NZ + z]
            yield e, (zz == z) & (c == e), src, dst, dev(zz, x, y, e)

    def attend(step):
        b = order[step]

        @pl.loop(0, 4, unroll=True)
        def _(i):
            zz = 2 * i + c
            block = (zz * NX + x) * 4 + b
            ids = [
                jnp.maximum(block - 1, 0),
                block,
                jnp.minimum(block + 1, 127),
                glob_ref[0],
                glob_ref[1],
                meta_s[zz, 0, 4 + b * 3],
                meta_s[zz, 0, 5 + b * 3],
                meta_s[zz, 0, 6 + b * 3],
            ]
            q = qbuf[i * 4 + b]
            keys = jnp.concatenate([kbuf[n] for n in ids], axis=0)
            scores = lax.dot_general(q, keys, (((1,), (1,)), ((), ())), preferred_element_type=F32)
            low = jnp.where(block > 0, 0.0, -1e30).astype(F32)
            high = jnp.where(block < 127, 0.0, -1e30).astype(F32)
            scores = jnp.concatenate(
                [
                    scores[:, :BLK] + low,
                    scores[:, BLK : 2 * BLK],
                    scores[:, 2 * BLK : 3 * BLK] + high,
                    scores[:, 3 * BLK :],
                ],
                axis=1,
            ) * SCORE_SCALE
            top = jnp.max(scores, axis=1, keepdims=True)
            weights = jnp.exp2(scores - top).astype(BF16)
            values = jnp.concatenate([vbuf[n] for n in ids], axis=0)
            both = jnp.dot(weights, jnp.concatenate([values, ones], axis=1), preferred_element_type=F32)
            osend[step, i] = (both[:, :HD] / both[:, HD:]).astype(BF16)
            for e, same, src, dst, to in o_copies(step, b, i):

                @pl.when(same)
                def _():
                    local(src, dst, o_recv.at[step]).start()

                @pl.when(jnp.logical_not(same))
                def _():
                    remote(src, dst, o_send.at[step, i, e], o_recv.at[step], to).start()

    def outputs_of(step):
        b = order[step]
        arrived(obuf.at[pl.ds(b * NZ, NZ)], o_recv.at[step])
        return b

    def project(b, first, last, finish):
        @pl.loop(first, last, unroll=True)
        def _(n):
            cols = pl.ds(pl.multiple_of(n * TILE, TILE), TILE)
            rows = jnp.concatenate([obuf[b * NZ + m] for m in range(NZ)], axis=1)
            finish(cols, jnp.dot(rows, wbuf[:, cols], preferred_element_type=F32))

    half = WIDTH // 2
    quarter = WIDTH // 4
    tiles = WIDTH // TILE
    left, right = pl.ds(0, half), pl.ds(half, half)

    def y_copy(k, src, dst, yy):
        return remote(src, dst, y_send.at[k], y_recv.at[k], dev(z, x, yy, c))

    y_copies = [
        y_copy(0, st1.at[:, pl.ds(0, quarter)], sa.at[:, pl.ds(0, quarter)], yr),
        y_copy(1, st1.at[:, pl.ds(half, quarter)], sb.at[:, pl.ds(0, quarter)], yl),
        y_copy(2, st2.at[:, right], ra.at[:, right], yr),
        y_copy(3, st2.at[:, left], ra.at[:, left], yr),
        y_copy(4, st3.at[:, left], rb.at[:, left], yl),
        y_copy(5, st3.at[:, right], rb.at[:, right], yl),
        y_copy(6, st1.at[:, pl.ds(quarter, quarter)], sa.at[:, pl.ds(quarter, quarter)], yr),
        y_copy(7, st1.at[:, pl.ds(half + quarter, quarter)], sb.at[:, pl.ds(quarter, quarter)], yl),
    ]

    def put(ref):
        def finish(cols, tile):
            ref[:, cols] = tile.astype(ref.dtype)

        return finish

    def project_0():
        b = outputs_of(0)
        for part, k in enumerate((0, 6, 1, 7)):
            project(b, part * tiles // 4, (part + 1) * tiles // 4, put(st1))
            y_copies[k].start()

    def project_1_near():
        b = outputs_of(1)
        project(b, tiles // 2, tiles, put(st2))

    def project_1_far():
        def finish(cols, tile):
            st2[:, cols] = (tile + sa[:, cols].astype(F32)).astype(BF16)

        y_copies[0].wait_recv()
        y_copies[6].wait_recv()
        project(order[1], 0, tiles // 2, finish)
        y_copies[3].start()

    def project_2_near():
        b = outputs_of(2)
        project(b, 0, tiles // 2, put(st3))

    def project_2_far():
        y_copies[1].wait_recv()
        y_copies[7].wait_recv()
        b = order[2]

        @pl.loop(tiles // 2, tiles, unroll=True)
        def _(n):
            cols = pl.ds(pl.multiple_of(n * TILE, TILE), TILE)
            near = pl.ds(pl.multiple_of(n * TILE - half, TILE), TILE)
            rows = jnp.concatenate([obuf[b * NZ + m] for m in range(NZ)], axis=1)
            tile = jnp.dot(rows, wbuf[:, cols], preferred_element_type=F32)
            st3[:, cols] = (tile + sb[:, near].astype(F32)).astype(BF16)

        y_copies[5].start()

    def project_3():
        b = outputs_of(3)
        project(b, 0, tiles, put(total))

    def first_phase_left():
        for cp in meta_z:
            cp.wait_send()
        for cp in meta_x:
            cp.wait_send()
        for j in range(4):
            for t in range(3):
                for h in range(CHUNKS[t]):
                    z_done(t, h, j)
        for t in range(2):

            @pl.loop(0, 4)
            def _(i):
                for h in range(CHUNKS[t]):
                    x_out(t, h, i, 0, xr, l_recv).wait_send()
                    x_out(t, h, i, 1, xl, r_recv).wait_send()
                    forward(t, h, i).wait_send()
                share(t, i).wait_send()

    attend(0)
    attend(1)
    keep_w.wait()
    copy_w.wait_send()
    arrived(wbuf.at[w_other], w_recv)
    attend(2)
    project_0()
    project_1_near()
    attend(3)
    first_phase_left()
    y_copies[0].wait_send()
    y_copies[6].wait_send()
    y_copies[2].start()
    project_2_near()
    y_copies[1].wait_send()
    y_copies[7].wait_send()
    y_copies[4].start()
    project_1_far()
    project_2_far()
    project_3()
    def add_up(first):
        for n in range(first, first + tiles // 2):
            cols = pl.ds(n * TILE, TILE)
            total[:, cols] = total[:, cols] + (ra if first else rb)[:, cols].astype(F32)

    def finish_half(first):
        for n in range(first, first + tiles // 2):
            cols = pl.ds(n * TILE, TILE)
            out_ref[:, cols] = (total[:, cols] + (rb if first else ra)[:, cols].astype(F32)).astype(BF16)

    for step in range(4):

        @pl.loop(0, 4)
        def _(i):
            for e, same, src, dst, to in o_copies(step, order[step], i):

                @pl.when(jnp.logical_not(same))
                def _():
                    remote(src, dst, o_send.at[step, i, e], o_recv.at[step], to).wait_send()

    y_copies[2].wait_recv()
    add_up(tiles // 2)
    y_copies[4].wait_recv()
    add_up(0)
    y_copies[3].wait_recv()
    finish_half(0)
    y_copies[5].wait_recv()
    finish_half(tiles // 2)

    for cp in y_copies[2:6]:
        cp.wait_send()


def on_device(q, k, v, w, doc_reset, rand_group, rand_slot, global_blocks):
    pair = np.arange(HD // 2, dtype=np.float64) * (2.0 / HD)
    freq = np.exp(-pair * math.log(ROPE_BASE)).astype(np.float32)
    freq = jnp.asarray(np.broadcast_to(np.concatenate([freq, freq])[None], (8, HD)).copy())
    deep = max(CHUNKS)
    vmem = pltpu.VMEM
    dma = pltpu.SemaphoreType.DMA
    any_spec = pl.BlockSpec(memory_space=pl.ANY)
    vmem_spec = pl.BlockSpec(memory_space=pltpu.VMEM)
    return pl.pallas_call(
        kernel,
        out_shape=jax.ShapeDtypeStruct((64, WIDTH), BF16),
        in_specs=[any_spec] * 4 + [vmem_spec] + [pl.BlockSpec(memory_space=pltpu.SMEM)] * 4,
        out_specs=vmem_spec,
        scratch_shapes=[
            vmem((8, HD), jnp.int32),
            vmem((GT, GT), BF16),
            vmem((GT, GT), BF16),
            vmem((4, 4, BLK, HD), BF16),
            vmem((4, 4, BLK, HD), BF16),
            vmem((16, BLK, HD), BF16),
            vmem((128, BLK, HD), BF16),
            vmem((128, BLK, HD), BF16),
            vmem((2 * GT, WIDTH), BF16),
            vmem((NX, NZ, 8, HD), jnp.int32),
            pltpu.SMEM((NZ, 8, HD), jnp.int32),
            vmem((GT, HD), F32),
            vmem((GT, HD), F32),
            vmem((4, 4, BLK, HD), BF16),
            vmem((4 * NZ, 64, HD), BF16),
            vmem((64, WIDTH), BF16),
            vmem((64, WIDTH), BF16),
            vmem((64, WIDTH), BF16),
            vmem((64, WIDTH // 2), BF16),
            vmem((64, WIDTH // 2), BF16),
            vmem((64, WIDTH), BF16),
            vmem((64, WIDTH), BF16),
            vmem((64, WIDTH), F32),
            dma((2,)), dma, dma, dma,
            dma((NZ - 1,)), dma((NZ - 1,)), dma((NX - 1,)), dma((NX - 1,)), dma,
            dma((3, deep, 4)), dma((3, deep, 4)), dma((2, deep, 4, 2)), dma((2, deep, 4)),
            dma((2, deep, 4)), dma((2, deep, 4)), dma((2, deep, 4)), dma((2, 4)), dma((2, 4)),
            dma((4, 4, 2)), dma((4,)), dma((8,)), dma((8,)),
        ],
        compiler_params=pltpu.CompilerParams(
            collective_id=0, has_side_effects=True, vmem_limit_bytes=63 << 20
        ),
        cost_estimate=pl.CostEstimate(flops=3_300_000_000, bytes_accessed=8 << 20, transcendentals=2_200_000),
    )(q, k, v.reshape(4, BLK, GT), w, freq, doc_reset, rand_group, rand_slot, global_blocks)


def solution(mesh):
    placed = (
        P("ctx", "head"),
        P("ctx", "head"),
        P("ctx", "head"),
        P("head", None),
        P("ctx"),
        P("ctx", None),
        P("ctx", None),
        P(),
    )
    return jax.shard_map(
        on_device, mesh=mesh, in_specs=placed, out_specs=P(("ctx", "head"), None), check_vma=False
    )
```

```python
import math

import jax
import jax.numpy as jnp
import numpy as np
from jax import lax
from jax.experimental import pallas as pl
from jax.experimental.pallas import tpu as pltpu
from jax.sharding import PartitionSpec as P

HD = 128
BLK = 128
NZ, NX, NY = 8, 4, 4
GT = 512
WIDTH = 4096
TILE = 512
CHUNKS = (2, 1, 1)
ROPE_BASE = 500000.0
MESH = pl.DeviceIdType.MESH
F32 = jnp.float32
BF16 = jnp.bfloat16
SCORE_SCALE = HD ** (-0.5) * math.log2(math.e)


def sin_cos(angle):
    turns = jnp.floor(angle * (2.0 / math.pi) + 0.5)
    r = angle - turns * 1.5703125
    r = r - turns * 4.837512969970703125e-4
    r = r - turns * 7.54978995489188216e-8
    quarter = turns - 4.0 * jnp.floor(turns * 0.25)
    z = r * r
    s = r + r * z * (-1.6666654611e-1 + z * (8.3321608736e-3 + z * -1.9515295891e-4))
    c = 1.0 - 0.5 * z + z * z * (
        4.166664568298827e-2 + z * (-1.388731625493765e-3 + z * 2.443315711809948e-5)
    )
    odd = (quarter == 1.0) | (quarter == 3.0)
    sine = jnp.where(odd, c, s)
    cosine = jnp.where(odd, s, c)
    sine = jnp.where(quarter >= 2.0, -sine, sine)
    cosine = jnp.where((quarter == 1.0) | (quarter == 2.0), -cosine, cosine)
    return sine, cosine


def code(*digits):
    return sum(d * 4**k for k, d in enumerate(digits))


def kernel(
    q_hbm, k_hbm, v_hbm, w_hbm, freq_ref, doc_ref, group_ref, slot_ref, glob_ref, out_ref,
    meta_ref, qin, kin, qrot, krot, qbuf, kbuf, vbuf, wbuf, mall, meta_s, cos_t, sin_t,
    osend, obuf, st1, st2, st3, sa, sb, ra, rb, total,
    in_sem, w_sem, w_send, w_recv,
    mz_send, mz_recv, mx_send, mx_recv, ms_sem,
    z_send, z_recv, x_send, f_send, l_recv, r_recv, f_recv, s_send, s_recv,
    o_send, o_recv, y_send, y_recv,
):
    ctx = lax.axis_index("ctx")
    head = lax.axis_index("head")
    z, x = ctx // NX, ctx % NX
    y, c = head // 2, head % 2
    xr, xl = (x + 1) % NX, (x + NX - 1) % NX
    yr, yl = (y + 1) % NY, (y + NY - 1) % NY
    yo = (y + 2) % NY
    xo = (x + 2) % NX

    def dev(zz, xx, yy, cc):
        return (zz * NX + xx, yy * 2 + cc)

    sib = dev(z, x, y, 1 - c)

    def local(src, dst, sem):
        return pltpu.make_async_copy(src, dst, sem)

    def remote(src, dst, ssem, rsem, to):
        return pltpu.make_async_remote_copy(
            src_ref=src, dst_ref=dst, send_sem=ssem, recv_sem=rsem, device_id=to, device_id_type=MESH
        )

    def arrived(dst, sem):
        pltpu.make_async_copy(dst, dst, sem).wait()

    copy_k = local(k_hbm, kin, in_sem.at[0])
    copy_q = local(q_hbm, qin, in_sem.at[1])
    copy_k.start()
    copy_q.start()

    numbers = [doc_ref[b] for b in range(4)]
    numbers += [group_ref[b, n] * 4 + slot_ref[b, n] for b in range(4) for n in range(3)]
    spot = lax.broadcasted_iota(jnp.int32, (8, HD), 1)
    packed = jnp.zeros((8, HD), jnp.int32)
    for n, number in enumerate(numbers):
        packed = jnp.where(spot == n, number, packed)
    meta_ref[...] = packed

    barrier = pltpu.get_barrier_semaphore()
    for d in range(NZ):
        for e in range(2):
            if d or e:
                pl.semaphore_signal(
                    barrier, inc=1, device_id=dev((z + d) % NZ, x, y, (c + e) % 2), device_id_type=MESH
                )
    for xx in (xr, xl, xo):
        pl.semaphore_signal(barrier, inc=1, device_id=dev(z, xx, y, c), device_id_type=MESH)
    for yy in (yr, yl):
        pl.semaphore_signal(barrier, inc=1, device_id=dev(z, x, yy, c), device_id_type=MESH)
    pl.semaphore_wait(barrier, 2 * NZ - 1 + 3 + 2)

    meta_z = []
    for d in range(1, NZ):
        cp = remote(meta_ref, mall.at[x, z], mz_send.at[d - 1], mz_recv.at[d - 1], dev((z + d) % NZ, x, y, c))
        cp.start()
        meta_z.append(cp)
    mall[x, z] = meta_ref[...]

    def chunk(base, t, h):
        size = 4 // CHUNKS[t]
        return pl.ds(base * 4 + h * size, size)

    target_core = z % 2

    place = z % 4
    near = jnp.where(
        place == 0, code(0, 1, 2, 3),
        jnp.where(place == 1, code(1, 0, 2, 3), jnp.where(place == 2, code(2, 3, 1, 0), code(3, 2, 1, 0))),
    )
    far = jnp.where(
        place == 0, code(3, 2, 1, 0),
        jnp.where(place == 1, code(3, 2, 0, 1), jnp.where(place == 2, code(0, 1, 3, 2), code(0, 1, 2, 3))),
    )
    targets = jnp.where(z // 4 == c, near, far)
    target = [(targets // 4**k) % 4 for k in range(4)]
    nearest = (z - c + 1) // 2 + 4
    sender = [(nearest + d) % 4 for d in (0, 3, 1, 2)]

    def z_piece(t, h, j):
        if t == 0:
            src = v_hbm.at[chunk(0, t, h), :, pl.ds(pl.multiple_of(j * HD, HD), HD)]
            return src, vbuf.at[chunk(ctx, t, h)]
        if t == 1:
            return krot.at[j, chunk(0, t, h)], kbuf.at[chunk(ctx, t, h)]
        return qrot.at[j, chunk(0, t, h)], qbuf.at[chunk(z // 2, t, h)]

    def z_start(t, h, j):
        row = 4 * c + j
        same = (row == z) & (target_core == c)
        src, dst = z_piece(t, h, j)
        send, recv = z_send.at[t, h, j], z_recv.at[t, h, z // 2]

        @pl.when(same)
        def _():
            local(src, dst, recv).start()

        @pl.when(jnp.logical_not(same))
        def _():
            remote(src, dst, send, recv, dev(row, x, y, target_core)).start()

    def z_done(t, h, j):
        row = 4 * c + j
        same = (row == z) & (target_core == c)
        src, dst = z_piece(t, h, j)

        @pl.when(jnp.logical_not(same))
        def _():
            remote(src, dst, z_send.at[t, h, j], z_recv.at[t, h, z // 2], dev(row, x, y, target_core)).wait_send()

    bufs = (vbuf, kbuf)

    def group_from(i, xx):
        return (2 * i + c) * NX + xx

    def x_out(t, h, i, k, to_x, recv):
        piece = bufs[t].at[chunk(group_from(i, x), t, h)]
        return remote(piece, piece, x_send.at[t, h, i, k], recv.at[t, h, i], dev(z, to_x, y, c))

    def row_blocks(i, core):
        return pl.ds((2 * i + core) * 4 * NX, 4 * NX)

    def share(t, i):
        piece = bufs[t].at[row_blocks(i, c)]
        return remote(piece, piece, s_send.at[t, i], s_recv.at[t, i], sib)

    def forward(t, h, i):
        from_x = jnp.where(c == 0, xl, xr)
        to_x = jnp.where(c == 0, xr, xl)
        piece = bufs[t].at[chunk(group_from(i, from_x), t, h)]
        return remote(piece, piece, f_send.at[t, h, i], f_recv.at[t, h, i], dev(z, to_x, y, c))

    def own_step(t, h, n):
        i = sender[n]
        arrived(bufs[t].at[chunk(group_from(i, x), t, h)], z_recv.at[t, h, i])
        x_out(t, h, i, 0, xr, l_recv).start()
        x_out(t, h, i, 1, xl, r_recv).start()

    def side_step(t, h, n):
        i = sender[n]
        arrived(bufs[t].at[chunk(group_from(i, xl), t, h)], l_recv.at[t, h, i])

        @pl.when(c == 0)
        def _():
            forward(t, h, i).start()

        arrived(bufs[t].at[chunk(group_from(i, xr), t, h)], r_recv.at[t, h, i])

        @pl.when(c == 1)
        def _():
            forward(t, h, i).start()


    def far_step(t, h, n):
        i = sender[n]
        arrived(bufs[t].at[chunk(group_from(i, xo), t, h)], f_recv.at[t, h, i])
        if h == CHUNKS[t] - 1:
            share(t, i).start()

    def z_chunk(t, h):
        if h < CHUNKS[t]:
            for j in target:
                z_start(t, h, j)

    z_chunk(0, 0)

    for cp in meta_z:
        cp.wait_recv()
    meta_x = []
    for d in range(1, NX):
        cp = remote(mall.at[x], mall.at[x], mx_send.at[d - 1], mx_recv.at[d - 1], dev(z, (x + d) % NX, y, c))
        cp.start()
        meta_x.append(cp)
    copy_s = local(mall.at[x], meta_s, ms_sem)
    copy_s.start()
    for n in range(4):
        own_step(0, 0, n)
        if n == 0:
            z_chunk(0, 1)
    for cp in meta_x:
        cp.wait_recv()

    doc = mall[:, :, 0, :].astype(F32)
    group_ids = lax.broadcasted_iota(jnp.int32, (NX, NZ, HD), 1) * NX + lax.broadcasted_iota(
        jnp.int32, (NX, NZ, HD), 0
    )
    lane = lax.broadcasted_iota(jnp.int32, (NX, NZ, HD), 2)
    block_ids = group_ids * 4 + lane
    starts = jnp.where((lane < 4) & (doc < float(BLK)), block_ids.astype(F32) * float(BLK) + doc, 0.0)
    own_doc = meta_ref[0:1, :].astype(F32)
    offset = lax.broadcasted_iota(jnp.int32, (BLK, HD), 0).astype(F32)
    half_sign = jnp.where(lax.broadcasted_iota(jnp.int32, (BLK, HD), 1) < HD // 2, -1.0, 1.0)
    for b in range(4):
        block = ctx * 4 + b
        before = jnp.where(block_ids < block, starts, 0.0)
        before = jnp.max(jnp.max(before, axis=0), axis=0, keepdims=True)
        before = jnp.max(before, axis=1, keepdims=True)
        reset = own_doc[0:1, b : b + 1]
        first = (block * BLK).astype(F32)
        begin = jnp.where(offset >= reset, first + reset, before)
        angle = (first + offset - begin) * freq_ref[0:1, :]
        sine, cosine = sin_cos(angle)
        cos_t[b * BLK : (b + 1) * BLK, :] = cosine
        sin_t[b * BLK : (b + 1) * BLK, :] = sine * half_sign

    def rotate(src, dst, j):
        for b in range(4):
            rows = pl.ds(b * BLK, BLK)
            value = src[rows, j * HD : (j + 1) * HD].astype(F32)
            turned = value * cos_t[rows, :] + pltpu.roll(value, HD // 2, 1) * sin_t[rows, :]
            dst[j, b] = turned.astype(BF16)

    copy_k.wait()
    for j in range(4):
        rotate(kin, krot, j)
    z_chunk(1, 0)
    for h in range(1, CHUNKS[0]):
        for n in range(4):
            own_step(0, h, n)
            if n == 0:
                z_chunk(0, h + 1)
            side_step(0, h - 1, n)
        if h == 1:
            copy_q.wait()
            for j in range(4):
                rotate(qin, qrot, j)
    w_rows = pl.ds(pl.multiple_of(c * GT, GT), GT)
    w_other = pl.ds(pl.multiple_of((1 - c) * GT, GT), GT)
    copy_w = remote(w_hbm, wbuf.at[w_rows], w_send, w_recv, sib)
    copy_w.start()
    keep_w = local(w_hbm, wbuf.at[w_rows], w_sem)
    keep_w.start()

    last = CHUNKS[0] - 1
    for h in range(CHUNKS[1]):
        for n in range(4):
            own_step(1, h, n)
            if n == 0:
                z_chunk(1, h + 1)
            if h == 0:
                side_step(0, last, n)
            else:
                side_step(1, h - 1, n)
    z_chunk(2, 0)
    for h in range(CHUNKS[0]):
        for n in range(4):
            if h == 0:
                side_step(1, CHUNKS[1] - 1, n)
            far_step(0, h, n)
    for h in range(CHUNKS[1]):
        for n in range(4):
            far_step(1, h, n)

    def from_sibling(t):
        @pl.loop(0, 4)
        def _(i):
            arrived(bufs[t].at[row_blocks(i, 1 - c)], s_recv.at[t, i])

    from_sibling(0)
    from_sibling(1)

    @pl.loop(0, 4)
    def _(i):
        for h in range(CHUNKS[2]):
            arrived(qbuf.at[chunk(i, 2, h)], z_recv.at[2, h, i])

    copy_s.wait()

    ones = jnp.ones((8 * BLK, HD), BF16)
    order = (yo, yr, yl, y)

    def o_copies(step, b, i):
        zz = 2 * i + c
        for e in range(2):
            src = osend.at[step, i, pl.ds(e * 64, 64)]
            dst = obuf.at[b * NZ + z]
            yield e, (zz == z) & (c == e), src, dst, dev(zz, x, y, e)

    def attend(step):
        b = order[step]

        @pl.loop(0, 4, unroll=True)
        def _(i):
            zz = 2 * i + c
            block = (zz * NX + x) * 4 + b
            ids = [
                jnp.maximum(block - 1, 0),
                block,
                jnp.minimum(block + 1, 127),
                glob_ref[0],
                glob_ref[1],
                meta_s[zz, 0, 4 + b * 3],
                meta_s[zz, 0, 5 + b * 3],
                meta_s[zz, 0, 6 + b * 3],
            ]
            q = qbuf[i * 4 + b]
            keys = jnp.concatenate([kbuf[n] for n in ids], axis=0)
            scores = lax.dot_general(q, keys, (((1,), (1,)), ((), ())), preferred_element_type=F32)
            low = jnp.where(block > 0, 0.0, -1e30).astype(F32)
            high = jnp.where(block < 127, 0.0, -1e30).astype(F32)
            scores = jnp.concatenate(
                [
                    scores[:, :BLK] + low,
                    scores[:, BLK : 2 * BLK],
                    scores[:, 2 * BLK : 3 * BLK] + high,
                    scores[:, 3 * BLK :],
                ],
                axis=1,
            ) * SCORE_SCALE
            top = jnp.max(scores, axis=1, keepdims=True)
            weights = jnp.exp2(scores - top).astype(BF16)
            values = jnp.concatenate([vbuf[n] for n in ids], axis=0)
            both = jnp.dot(weights, jnp.concatenate([values, ones], axis=1), preferred_element_type=F32)
            osend[step, i] = (both[:, :HD] / both[:, HD:]).astype(BF16)
            for e, same, src, dst, to in o_copies(step, b, i):

                @pl.when(same)
                def _():
                    local(src, dst, o_recv.at[step]).start()

                @pl.when(jnp.logical_not(same))
                def _():
                    remote(src, dst, o_send.at[step, i, e], o_recv.at[step], to).start()

    def outputs_of(step):
        b = order[step]
        arrived(obuf.at[pl.ds(b * NZ, NZ)], o_recv.at[step])
        return b

    def project(b, first, last, finish):
        @pl.loop(first, last, unroll=True)
        def _(n):
            cols = pl.ds(pl.multiple_of(n * TILE, TILE), TILE)
            rows = jnp.concatenate([obuf[b * NZ + m] for m in range(NZ)], axis=1)
            finish(cols, jnp.dot(rows, wbuf[:, cols], preferred_element_type=F32))

    half = WIDTH // 2
    quarter = WIDTH // 4
    tiles = WIDTH // TILE
    left, right = pl.ds(0, half), pl.ds(half, half)

    def y_copy(k, src, dst, yy):
        return remote(src, dst, y_send.at[k], y_recv.at[k], dev(z, x, yy, c))

    y_copies = [
        y_copy(0, st1.at[:, pl.ds(0, quarter)], sa.at[:, pl.ds(0, quarter)], yr),
        y_copy(1, st1.at[:, pl.ds(half, quarter)], sb.at[:, pl.ds(0, quarter)], yl),
        y_copy(2, st2.at[:, right], ra.at[:, right], yr),
        y_copy(3, st2.at[:, pl.ds(0, quarter)], ra.at[:, pl.ds(0, quarter)], yr),
        y_copy(4, st3.at[:, left], rb.at[:, left], yl),
        y_copy(5, st3.at[:, right], rb.at[:, right], yl),
        y_copy(6, st1.at[:, pl.ds(quarter, quarter)], sa.at[:, pl.ds(quarter, quarter)], yr),
        y_copy(7, st1.at[:, pl.ds(half + quarter, quarter)], sb.at[:, pl.ds(quarter, quarter)], yl),
        y_copy(8, st2.at[:, pl.ds(quarter, quarter)], ra.at[:, pl.ds(quarter, quarter)], yr),
    ]

    def put(ref):
        def finish(cols, tile):
            ref[:, cols] = tile.astype(ref.dtype)

        return finish

    def project_0():
        b = outputs_of(0)
        for part, k in enumerate((0, 6, 1, 7)):
            project(b, part * tiles // 4, (part + 1) * tiles // 4, put(st1))
            y_copies[k].start()

    def project_1_near():
        b = outputs_of(1)
        project(b, tiles // 2, tiles, put(st2))

    def project_1_far():
        def finish(cols, tile):
            st2[:, cols] = (tile + sa[:, cols].astype(F32)).astype(BF16)

        for part, came, out in ((0, 0, 3), (1, 6, 8)):
            y_copies[came].wait_recv()
            project(order[1], part * tiles // 4, (part + 1) * tiles // 4, finish)
            y_copies[out].start()

    def project_2_near():
        b = outputs_of(2)
        project(b, 0, tiles // 2, put(st3))

    def project_2_far():
        y_copies[1].wait_recv()
        y_copies[7].wait_recv()
        b = order[2]

        @pl.loop(tiles // 2, tiles, unroll=True)
        def _(n):
            cols = pl.ds(pl.multiple_of(n * TILE, TILE), TILE)
            near = pl.ds(pl.multiple_of(n * TILE - half, TILE), TILE)
            rows = jnp.concatenate([obuf[b * NZ + m] for m in range(NZ)], axis=1)
            tile = jnp.dot(rows, wbuf[:, cols], preferred_element_type=F32)
            st3[:, cols] = (tile + sb[:, near].astype(F32)).astype(BF16)

        y_copies[5].start()

    def project_3():
        b = outputs_of(3)
        project(b, 0, tiles, put(total))

    def first_phase_left():
        for cp in meta_z:
            cp.wait_send()
        for cp in meta_x:
            cp.wait_send()
        for j in range(4):
            for t in range(3):
                for h in range(CHUNKS[t]):
                    z_done(t, h, j)
        for t in range(2):

            @pl.loop(0, 4)
            def _(i):
                for h in range(CHUNKS[t]):
                    x_out(t, h, i, 0, xr, l_recv).wait_send()
                    x_out(t, h, i, 1, xl, r_recv).wait_send()
                    forward(t, h, i).wait_send()
                share(t, i).wait_send()

    attend(0)
    attend(1)
    keep_w.wait()
    copy_w.wait_send()
    arrived(wbuf.at[w_other], w_recv)
    attend(2)
    project_0()
    project_1_near()
    attend(3)
    first_phase_left()
    y_copies[0].wait_send()
    y_copies[6].wait_send()
    y_copies[2].start()
    project_2_near()
    y_copies[1].wait_send()
    y_copies[7].wait_send()
    y_copies[4].start()
    project_1_far()
    project_2_far()
    project_3()
    def add_up(first):
        for n in range(first, first + tiles // 2):
            cols = pl.ds(n * TILE, TILE)
            total[:, cols] = total[:, cols] + (ra if first else rb)[:, cols].astype(F32)

    def finish_half(first):
        for n in range(first, first + tiles // 2):
            cols = pl.ds(n * TILE, TILE)
            out_ref[:, cols] = (total[:, cols] + (rb if first else ra)[:, cols].astype(F32)).astype(BF16)

    for step in range(4):

        @pl.loop(0, 4)
        def _(i):
            for e, same, src, dst, to in o_copies(step, order[step], i):

                @pl.when(jnp.logical_not(same))
                def _():
                    remote(src, dst, o_send.at[step, i, e], o_recv.at[step], to).wait_send()

    y_copies[2].wait_recv()
    add_up(tiles // 2)
    y_copies[4].wait_recv()
    add_up(0)
    y_copies[3].wait_recv()
    y_copies[8].wait_recv()
    finish_half(0)
    y_copies[5].wait_recv()
    finish_half(tiles // 2)

    for cp in y_copies[2:6] + y_copies[8:]:
        cp.wait_send()


def on_device(q, k, v, w, doc_reset, rand_group, rand_slot, global_blocks):
    pair = np.arange(HD // 2, dtype=np.float64) * (2.0 / HD)
    freq = np.exp(-pair * math.log(ROPE_BASE)).astype(np.float32)
    freq = jnp.asarray(np.broadcast_to(np.concatenate([freq, freq])[None], (8, HD)).copy())
    deep = max(CHUNKS)
    vmem = pltpu.VMEM
    dma = pltpu.SemaphoreType.DMA
    any_spec = pl.BlockSpec(memory_space=pl.ANY)
    vmem_spec = pl.BlockSpec(memory_space=pltpu.VMEM)
    return pl.pallas_call(
        kernel,
        out_shape=jax.ShapeDtypeStruct((64, WIDTH), BF16),
        in_specs=[any_spec] * 4 + [vmem_spec] + [pl.BlockSpec(memory_space=pltpu.SMEM)] * 4,
        out_specs=vmem_spec,
        scratch_shapes=[
            vmem((8, HD), jnp.int32),
            vmem((GT, GT), BF16),
            vmem((GT, GT), BF16),
            vmem((4, 4, BLK, HD), BF16),
            vmem((4, 4, BLK, HD), BF16),
            vmem((16, BLK, HD), BF16),
            vmem((128, BLK, HD), BF16),
            vmem((128, BLK, HD), BF16),
            vmem((2 * GT, WIDTH), BF16),
            vmem((NX, NZ, 8, HD), jnp.int32),
            pltpu.SMEM((NZ, 8, HD), jnp.int32),
            vmem((GT, HD), F32),
            vmem((GT, HD), F32),
            vmem((4, 4, BLK, HD), BF16),
            vmem((4 * NZ, 64, HD), BF16),
            vmem((64, WIDTH), BF16),
            vmem((64, WIDTH), BF16),
            vmem((64, WIDTH), BF16),
            vmem((64, WIDTH // 2), BF16),
            vmem((64, WIDTH // 2), BF16),
            vmem((64, WIDTH), BF16),
            vmem((64, WIDTH), BF16),
            vmem((64, WIDTH), F32),
            dma((2,)), dma, dma, dma,
            dma((NZ - 1,)), dma((NZ - 1,)), dma((NX - 1,)), dma((NX - 1,)), dma,
            dma((3, deep, 4)), dma((3, deep, 4)), dma((2, deep, 4, 2)), dma((2, deep, 4)),
            dma((2, deep, 4)), dma((2, deep, 4)), dma((2, deep, 4)), dma((2, 4)), dma((2, 4)),
            dma((4, 4, 2)), dma((4,)), dma((9,)), dma((9,)),
        ],
        compiler_params=pltpu.CompilerParams(
            collective_id=0, has_side_effects=True, vmem_limit_bytes=63 << 20
        ),
        cost_estimate=pl.CostEstimate(flops=3_300_000_000, bytes_accessed=8 << 20, transcendentals=2_200_000),
    )(q, k, v.reshape(4, BLK, GT), w, freq, doc_reset, rand_group, rand_slot, global_blocks)


def solution(mesh):
    placed = (
        P("ctx", "head"),
        P("ctx", "head"),
        P("ctx", "head"),
        P("head", None),
        P("ctx"),
        P("ctx", None),
        P("ctx", None),
        P(),
    )
    return jax.shard_map(
        on_device, mesh=mesh, in_specs=placed, out_specs=P(("ctx", "head"), None), check_vma=False
    )
```
